256 devices in a mesh: seq: 32 (over y, z), row: 2 (over x_hi), col: 4 (over x_lo, core).
Axes of the slice: x: 4 (x_hi: 2, x_lo: 2; x = x_hi * 2 + x_lo), y: 4, z: 8, core: 2. Of those that a mesh axis runs over, the one named last changes fastest.
Arguments:
- tokens: bfloat16 [8192, 12288], P('seq', ('row', 'col')), may hold values from -24 to 24
- input_weight: bfloat16 [12288, 1536], P('row', 'col'), may hold values from -0.078125 to 0.078125
- output_weight: bfloat16 [512, 12288], P('col'), may hold values from -0.25 to 0.25
- output_cotangent: bfloat16 [8192, 12288], P(('seq', 'row'), 'col'), may hold values from -1.1953125 to 1.1953125
Outputs:
- layer_output: bfloat16 [8192, 12288], P(('seq', 'row'), 'col')
- input_grad: bfloat16 [8192, 12288], P('seq', ('row', 'col'))
The draws below stay inside these ranges and needn't reach their ends.
All inputs are finite; a program needn't handle non-finite values.
Results may differ from the reference program's by a relative error of at most 0.0364.
The reference program's roundings to bfloat16 on the way (of `packed`, `weights`, `attended`, `upstream`, `score_grad` and `packed_grad`) count: a program that leaves them out, or rounds other values in their place, can miss the bound.
Values may be sent and summed in bfloat16 or wider, within the bound.
A program may use at most 128 MiB of HBM per device.

```python
import math
import jax
import jax.numpy as jnp
from jax import lax

D = 12288
HEAD = 128
HEADS = 4
TOKENS = 8192


def draw_tokens(key, part):
    key = jax.random.fold_in(key, 7)
    first = jax.random.fold_in(key, 0)
    values = jnp.clip(jax.random.normal(first, (TOKENS, D), jnp.float32), -6.0, 6.0)
    return values.astype(jnp.bfloat16)


def shard_levels(key, dims, pieces, least, top_value):
    def one(dim, blocks):
        draws = jax.random.uniform(jax.random.fold_in(jax.random.fold_in(key, 6), dim), (blocks,), jnp.float32, least / len(pieces), top_value / len(pieces))
        return jnp.repeat(jnp.exp(draws), dims[dim] // blocks).reshape((-1,) + (1,) * (len(dims) - dim - 1))

    gain = one(*pieces[0])
    for cut in pieces[1:]:
        gain = gain * one(*cut)
    return gain


def gaussian(rng, shape, deviation, bound, cuts=(), held_as=jnp.bfloat16):
    entries = deviation * jax.random.normal(rng, shape, jnp.float32)
    if cuts:
        entries = entries * shard_levels(rng, shape, cuts, -0.22, 0.18)
    return jnp.clip(entries, -bound, bound).astype(held_as)


def setup_inputs(seed: int = 0) -> dict:
    splits = jax.random.split(jax.random.key(seed), 5)
    tokens = draw_tokens(jax.random.fold_in(splits[4], 71), 0)
    input_weight = gaussian(splits[1], (D, 3 * HEADS * HEAD), (D // 2) ** -0.5, 0.078125, ((0, 2), (1, 4)))
    output_weight = gaussian(splits[2], (HEADS * HEAD, D), (HEADS * HEAD) ** -0.5, 0.25, ((0, 4),))
    output_cotangent = gaussian(splits[3], (TOKENS, D), 0.2, 1.1953125, ((0, 64), (1, 4)))
    return dict(tokens=tokens, input_weight=input_weight, output_weight=output_weight, output_cotangent=output_cotangent)


masked_score = -1e+30

def split_heads(packed, which):
    shaped = packed.reshape(packed.shape[0], HEADS, 3, HEAD)
    return jnp.transpose(shaped[:, :, which, :], (1, 0, 2))

def reference(tokens, input_weight, output_weight, output_cotangent):
    factor = 1.0 / math.sqrt(HEAD)
    packed = jnp.dot(tokens, input_weight, preferred_element_type=jnp.float32).astype(jnp.bfloat16)
    queries = split_heads(packed, 0)
    keys_all = split_heads(packed, 1)
    values = split_heads(packed, 2)
    block_rows = math.gcd(TOKENS, 512)
    block_count = TOKENS // block_rows
    key_pos = jnp.arange(TOKENS, dtype=jnp.int32)

    def masked_scores(query_blk, begin_at):
        scores = jnp.einsum('hqd,hkd->hqk', query_blk.astype(jnp.float32), keys_all.astype(jnp.float32)) * factor
        query_pos = begin_at + jnp.arange(block_rows, dtype=jnp.int32)
        allowed = key_pos[None, :] <= query_pos[:, None]
        return jnp.where(allowed[None], scores, masked_score)

    def forward_block(block_index):
        begin_at = (block_index * block_rows).astype(jnp.int32)
        query_blk = lax.dynamic_slice_in_dim(queries, begin_at, block_rows, 1)
        scores = masked_scores(query_blk, begin_at)
        largest = lax.optimization_barrier(jnp.max(scores, axis=-1))
        weights = jnp.exp(scores - largest[..., None])
        total_sum = lax.optimization_barrier(jnp.sum(weights, axis=-1))
        low_weights = lax.optimization_barrier(weights.astype(jnp.bfloat16)).astype(jnp.float32)
        mixed_sum = jnp.einsum('hqk,hkd->hqd', low_weights, values.astype(jnp.float32))
        attended = (mixed_sum / total_sum[..., None]).astype(jnp.bfloat16)
        return (attended, largest + jnp.log(total_sum))
    attended, logsum = lax.map(forward_block, jnp.arange(block_count, dtype=jnp.int32))
    attended = jnp.transpose(attended, (1, 0, 2, 3)).reshape(HEADS, TOKENS, HEAD)
    logsum = jnp.transpose(logsum, (1, 0, 2)).reshape(HEADS, TOKENS)
    flattened = jnp.transpose(attended, (1, 0, 2)).reshape(TOKENS, HEADS * HEAD)
    layer_output = jnp.dot(flattened, output_weight, preferred_element_type=jnp.float32).astype(jnp.bfloat16)
    upstream = lax.dot_general(output_cotangent, output_weight, (((1,), (1,)), ((), ())), preferred_element_type=jnp.float32).astype(jnp.bfloat16)
    upstream = jnp.transpose(upstream.reshape(TOKENS, HEADS, HEAD), (1, 0, 2))
    row_delta = lax.optimization_barrier(jnp.sum(upstream.astype(jnp.float32) * attended.astype(jnp.float32), axis=-1))

    def backward_block(carry, block_index):
        key_grad, value_grad = carry
        begin_at = (block_index * block_rows).astype(jnp.int32)
        query_blk = lax.dynamic_slice_in_dim(queries, begin_at, block_rows, 1)
        upstream_blk = lax.dynamic_slice_in_dim(upstream, begin_at, block_rows, 1).astype(jnp.float32)
        logsum_blk = lax.dynamic_slice_in_dim(logsum, begin_at, block_rows, 1)
        delta_blk = lax.dynamic_slice_in_dim(row_delta, begin_at, block_rows, 1)
        scores = masked_scores(query_blk, begin_at)
        probabilities = jnp.exp(scores - logsum_blk[..., None])
        prob_grad = jnp.einsum('hqd,hkd->hqk', upstream_blk, values.astype(jnp.float32))
        score_grad = lax.optimization_barrier((probabilities * (prob_grad - delta_blk[..., None])).astype(jnp.bfloat16)).astype(jnp.float32)
        low_probs = lax.optimization_barrier(probabilities.astype(jnp.bfloat16)).astype(jnp.float32)
        query_grad = jnp.einsum('hqk,hkd->hqd', score_grad, keys_all.astype(jnp.float32))
        key_grad = key_grad + jnp.einsum('hqk,hqd->hkd', score_grad, query_blk.astype(jnp.float32))
        value_grad = value_grad + jnp.einsum('hqk,hqd->hkd', low_probs, upstream_blk)
        return ((key_grad, value_grad), query_grad)
    empty_grads = jnp.zeros((HEADS, TOKENS, HEAD), jnp.float32)
    (key_grad, value_grad), query_grad = lax.scan(backward_block, (empty_grads, empty_grads), jnp.arange(block_count, dtype=jnp.int32))
    query_grad = jnp.transpose(query_grad, (1, 0, 2, 3)).reshape(HEADS, TOKENS, HEAD)
    stacked = jnp.stack([query_grad * factor, key_grad * factor, value_grad], axis=0)
    packed_grad = jnp.transpose(stacked, (2, 1, 0, 3)).reshape(TOKENS, 3 * HEADS * HEAD).astype(jnp.bfloat16)
    input_grad = lax.dot_general(packed_grad, input_weight, (((1,), (1,)), ((), ())), preferred_element_type=jnp.float32).astype(jnp.bfloat16)
    return (layer_output, input_grad)
```

```python
import functools
import math

import jax
import jax.numpy as jnp
from jax import lax
from jax.experimental import pallas as pl
from jax.experimental.pallas import tpu as pltpu
from jax.sharding import PartitionSpec as P

HEAD = 128
MESH = pl.DeviceIdType.MESH
masked_score = -1e30
BF = jnp.bfloat16
F32 = jnp.float32
NJ = 4


def remote(src, dst, send_sem, recv_sem, device):
    return pltpu.make_async_remote_copy(
        src_ref=src,
        dst_ref=dst,
        send_sem=send_sem,
        recv_sem=recv_sem,
        device_id=device,
        device_id_type=MESH,
    )


def greet(devices):
    barrier = pltpu.get_barrier_semaphore()
    for device in devices:
        pl.semaphore_signal(barrier, inc=1, device_id=device, device_id_type=MESH)
    pl.semaphore_wait(barrier, len(devices))


def dot_nt(a, b):
    return lax.dot_general(a, b, (((1,), (1,)), ((), ())), preferred_element_type=F32)


def dot_tn(a, b):
    return lax.dot_general(a, b, (((0,), (0,)), ((), ())), preferred_element_type=F32)


def flip(c, bits):
    low, high = lax.rem(c, 2), c // 2
    if bits & 1:
        low = 1 - low
    if bits & 2:
        high = 1 - high
    return high * 2 + low


def seed_kernel(ns, w_ref, wo_ref, sw_ref, swo_ref, bw, bwo, send, recv):
    s, r, c = lax.axis_index("seq"), lax.axis_index("row"), lax.axis_index("col")
    depth = w_ref.shape[0] // 4
    piece = depth // ns
    width = wo_ref.shape[1] // 4
    part = width // NJ
    ni = ns // NJ
    rows = HEAD // ni
    j, i = s // ni, lax.rem(s, ni)
    peers = [flip(c, 2), flip(c, 3)]
    greet([(s, r, p) for p in peers])
    copies = []
    for h, p in enumerate(peers):
        copies.append(
            remote(
                w_ref.at[pl.ds(pl.multiple_of(p * depth + s * piece, 16), piece), :],
                bw.at[h],
                send.at[0, h],
                recv.at[0, h],
                (s, r, p),
            )
        )
        copies.append(
            remote(
                wo_ref.at[
                    pl.ds(pl.multiple_of(i * rows, 16), rows),
                    pl.ds(pl.multiple_of(p * width + j * part, 128), part),
                ],
                bwo.at[h],
                send.at[1, h],
                recv.at[1, h],
                (s, r, p),
            )
        )
    for copy in copies:
        copy.start()
    for copy in copies:
        copy.wait()
    n = bw.shape[2]
    for h in range(2):
        sw_ref[:, h * n : (h + 1) * n] = bw[h]
        swo_ref[:, h * part : (h + 1) * part] = bwo[h]


def seeds(w, wo):
    ns = lax.axis_size("seq")
    depth, n = w.shape[0] // 4, w.shape[1]
    part = wo.shape[1] // 4 // NJ
    rows = HEAD // (ns // NJ)
    vm = pl.BlockSpec(memory_space=pltpu.VMEM)
    return pl.pallas_call(
        functools.partial(seed_kernel, ns),
        out_shape=(
            jax.ShapeDtypeStruct((depth // ns, 2 * n), BF),
            jax.ShapeDtypeStruct((rows, 2 * part), BF),
        ),
        in_specs=[pl.BlockSpec(memory_space=pl.ANY)] * 2,
        out_specs=(vm, vm),
        scratch_shapes=[
            pltpu.VMEM((2, depth // ns, n), BF),
            pltpu.VMEM((2, rows, part), BF),
            pltpu.SemaphoreType.DMA((2, 2)),
            pltpu.SemaphoreType.DMA((2, 2)),
        ],
        compiler_params=pltpu.CompilerParams(collective_id=0, has_side_effects=True),
        name="seeds",
    )(w, wo)


CHUNKS = 4


def proj_kernel(
    t_ref, w_ref, packed_ref, wsib_ref, tbuf, wv, psend, precv, wsem, lsem, sib, snd, rcv, psnd, prcv
):
    s, r, c = lax.axis_index("seq"), lax.axis_index("row"), lax.axis_index("col")
    depth = t_ref.shape[1]
    half = t_ref.shape[0] // 2
    step = 2 * half // CHUNKS
    sibling, across, far = flip(c, 1), flip(c, 2), flip(c, 3)
    to_sib, to_across, to_row = (s, r, sibling), (s, r, across), (s, 1 - r, c)

    wcopy = pltpu.make_async_copy(w_ref, wv, wsem)
    wcopy.start()

    def rows_of(k):
        hk = CHUNKS // 2
        start = (1 - r) * half + k * step if k < hk else r * half + (k - hk) * step
        return pl.ds(pl.multiple_of(start, step), step)

    own = pltpu.make_async_copy(t_ref, tbuf.at[c], lsem)
    own.start()
    greet([to_sib, to_across, to_row])

    def token_copy(kind, k):
        rows = rows_of(k)
        if kind == 0:
            return remote(t_ref.at[rows], tbuf.at[c, rows], snd.at[0, k], rcv.at[0, k], to_across)
        if kind == 1:
            return remote(t_ref.at[rows], tbuf.at[c, rows], snd.at[1, k], rcv.at[1, k], to_sib)
        return remote(
            tbuf.at[across, rows], tbuf.at[across, rows], snd.at[2, k], rcv.at[2, k], to_sib
        )

    def arrival(kind, k):
        rows = rows_of(k)
        slot = (across, sibling, far)[kind]
        return remote(
            tbuf.at[slot, rows], tbuf.at[slot, rows], snd.at[kind, k], rcv.at[kind, k], to_sib
        )

    for k in range(CHUNKS):
        token_copy(0, k).start()
        token_copy(1, k).start()
    wide = remote(
        w_ref.at[pl.ds(pl.multiple_of(sibling * depth, 16), depth), :],
        wsib_ref,
        sib.at[0],
        sib.at[1],
        to_sib,
    )
    wide.start()
    own.wait()
    wcopy.wait()

    def product(slot, rows):
        return jnp.dot(
            tbuf[slot, rows, :],
            wv[pl.ds(pl.multiple_of(slot * depth, 16), depth), :],
            preferred_element_type=F32,
        )

    def part_copy(k):
        rows = pl.ds(k * step, step)
        return remote(psend.at[rows], precv.at[rows], psnd.at[k], prcv.at[k], to_row)

    for k in range(CHUNKS):
        rows = rows_of(k)
        arrival(0, k).wait_recv()
        token_copy(2, k).start()
        arrival(1, k).wait_recv()
        acc = product(c, rows) + product(sibling, rows) + product(across, rows)
        arrival(2, k).wait_recv()
        acc = acc + product(far, rows)
        hk = CHUNKS // 2
        if k < hk:
            psend[pl.ds(k * step, step), :] = acc
            part_copy(k).start()
        else:
            part_copy(k - hk).wait_recv()
            out = pl.ds((k - hk) * step, step)
            packed_ref[out, :] = (acc + precv[out, :]).astype(BF)
    for k in range(CHUNKS):
        for kind in range(3):
            token_copy(kind, k).wait_send()
    for k in range(CHUNKS // 2):
        part_copy(k).wait_send()
    wide.wait()


def project(tokens, w):
    rows, depth = tokens.shape
    n = w.shape[1]
    half = rows // 2
    hbm = pl.BlockSpec(memory_space=pl.ANY)
    return pl.pallas_call(
        proj_kernel,
        out_shape=(
            jax.ShapeDtypeStruct((half, n), BF),
            jax.ShapeDtypeStruct((depth, n), BF),
        ),
        in_specs=[hbm, hbm],
        out_specs=(pl.BlockSpec(memory_space=pltpu.VMEM), hbm),
        scratch_shapes=[
            pltpu.VMEM((4, rows, depth), BF),
            pltpu.VMEM(w.shape, BF),
            pltpu.VMEM((half, n), F32),
            pltpu.VMEM((half, n), F32),
            pltpu.SemaphoreType.DMA,
            pltpu.SemaphoreType.DMA,
            pltpu.SemaphoreType.DMA((2,)),
            pltpu.SemaphoreType.DMA((3, CHUNKS)),
            pltpu.SemaphoreType.DMA((3, CHUNKS)),
            pltpu.SemaphoreType.DMA((CHUNKS // 2,)),
            pltpu.SemaphoreType.DMA((CHUNKS // 2,)),
        ],
        compiler_params=pltpu.CompilerParams(
            collective_id=1, has_side_effects=True, vmem_limit_bytes=40 * 2**20
        ),
        cost_estimate=pl.CostEstimate(
            flops=2 * rows * 4 * depth * n, bytes_accessed=60_000_000, transcendentals=0
        ),
        name="project",
    )(tokens, w)


def attention_kernel(
    ny,
    nz,
    packed_ref,
    do_ref,
    wo_ref,
    woth_ref,
    out_ref,
    dp_ref,
    q_all,
    kv_all,
    u_all,
    do_v,
    wo_v,
    ups,
    upr,
    s_all,
    o_snd,
    o_rcv,
    st_snd,
    st_rcv,
    ld_snd,
    ld_rcv,
    att_all,
    dq_acc,
    dq_snd,
    dq_rcv,
    dkv_own,
    dkv_snd,
    dkv_rcv,
    row_snd,
    row_rcv,
    dp_all,
    lsem,
    zs,
    zr,
    kvs,
    kvr,
    cs,
    cr,
    ds,
    dr,
    gs,
    gr,
):
    s, r, c = lax.axis_index("seq"), lax.axis_index("row"), lax.axis_index("col")
    y, z = s // nz, lax.rem(s, nz)
    factor = 1.0 / math.sqrt(HEAD)
    width = do_ref.shape[1]
    part = width // NJ
    sibling, across, far = flip(c, 1), flip(c, 2), flip(c, 3)
    cols = [sibling, across, far]
    slab = 2 * HEAD

    def at_z(d):
        return lax.rem(z + d + nz, nz)

    def dev_z(d):
        return (y * nz + at_z(d), r, c)

    def dev_y(yy):
        return (yy * nz + z, r, c)

    to_row = (s, 1 - r, c)
    to_cols = [(s, r, p) for p in cols]
    to_diag = (s, 1 - r, across)

    loads = [
        pltpu.make_async_copy(do_ref, do_v, lsem.at[0]),
        pltpu.make_async_copy(
            wo_ref.at[:, pl.ds(pl.multiple_of(c * width, 128), width)], wo_v.at[c], lsem.at[1]
        ),
    ]
    for j in range(NJ):
        for h, p in enumerate((across, far)):
            loads.append(
                pltpu.make_async_copy(
                    woth_ref.at[pl.ds(j * HEAD, HEAD), pl.ds(h * part, part)],
                    wo_v.at[p, :, pl.ds(j * part, part)],
                    lsem.at[2 + 2 * j + h],
                )
            )
    for load in loads:
        load.start()

    def z_rows(zz):
        return pl.ds(pl.multiple_of(zz * HEAD, HEAD), HEAD)

    def kv_rows(yy, rr):
        return pl.ds(pl.multiple_of(yy * slab + rr * HEAD, HEAD), HEAD)

    q_all[z_rows(z), :] = packed_ref[:, :HEAD]
    kv_all[kv_rows(y, r), :] = packed_ref[:, HEAD:]

    greet(
        [dev_z(d) for d in range(1, nz)]
        + [(lax.rem(y + d, ny) * nz + z, r, c) for d in range(1, ny)]
        + [to_row]
        + to_cols
        + [to_diag]
    )

    def kv_row():
        rows = kv_rows(y, r)
        return remote(kv_all.at[rows], kv_all.at[rows], kvs.at[0], kvr.at[2 * ny], to_row)

    def kv_row_arrival():
        rows = kv_rows(y, 1 - r)
        return remote(kv_all.at[rows], kv_all.at[rows], kvs.at[0], kvr.at[2 * ny], to_row)

    def kv_send(d, other):
        rr = 1 - r if other else r
        rows = kv_rows(y, rr)
        return remote(
            kv_all.at[rows],
            kv_all.at[rows],
            kvs.at[1 + 2 * d + other],
            kvr.at[2 * y + other],
            dev_y(lax.rem(y + d, ny)),
        )

    def kv_arrival(yy, other):
        rr = 1 - r if other else r
        rows = kv_rows(yy, rr)
        return remote(kv_all.at[rows], kv_all.at[rows], kvs.at[0], kvr.at[2 * yy + other], to_row)

    kv_row().start()
    for d in range(1, ny):

        @pl.when(y + d < ny)
        def _():
            kv_send(d, 0).start()

    def z_gather(kind, buf, d):
        return remote(buf.at[z_rows(z)], buf.at[z_rows(z)], zs.at[kind, d], zr.at[kind, d], dev_z(d))

    def z_gather_arrival(kind, buf, d):
        rows = z_rows(at_z(-d))
        return remote(buf.at[rows], buf.at[rows], zs.at[kind, d], zr.at[kind, d], dev_z(d))

    def z_give(kind, src, dst, d):
        return remote(src.at[at_z(d)], dst.at[z], zs.at[kind, d], zr.at[kind, d], dev_z(d))

    def z_give_arrival(kind, dst, d):
        slot = at_z(-d)
        return remote(dst.at[slot], dst.at[slot], zs.at[kind, d], zr.at[kind, d], dev_z(d))

    order = sorted(range(1, nz), key=lambda d: -min(d, nz - d))
    for d in order:
        z_gather(0, q_all, d).start()

    wo_sib = remote(
        wo_ref.at[:, pl.ds(pl.multiple_of(sibling * width, 128), width)],
        wo_v.at[c],
        cs.at[0, 0],
        cr.at[0, 0],
        to_cols[0],
    )
    wo_sib.start()
    wo_sib_in = remote(wo_v.at[sibling], wo_v.at[sibling], cs.at[0, 0], cr.at[0, 0], to_cols[0])

    kv_row_arrival().wait_recv()
    for d in range(1, ny):

        @pl.when(y + d < ny)
        def _():
            kv_send(d, 1).start()

    for load in loads:
        load.wait()
    wo_sib_in.wait_recv()
    ups_copies = []
    for h, p in enumerate(cols):
        ups[p] = dot_nt(do_v[...], wo_v[p])
        copy = remote(ups.at[p], upr.at[c], cs.at[1, h], cr.at[1, h], to_cols[h])
        copy.start()
        ups_copies.append(copy)
    upr[c] = dot_nt(do_v[...], wo_v[c])

    for d in order:
        z_gather_arrival(0, q_all, d).wait_recv()
    nq = nz * HEAD
    lane = lax.broadcasted_iota(jnp.int32, (1, nq), 1)
    qpos = (y * nz + lane // HEAD) * slab + r * HEAD + lane % HEAD
    kofs = lax.broadcasted_iota(jnp.int32, (slab, 1), 0)

    def y_rows(yy):
        return pl.ds(pl.multiple_of(yy * slab, slab), slab)

    def score_turn(yy, largest):
        @pl.when(yy < y)
        def _():
            kv_arrival(yy, 0).wait_recv()
            kv_arrival(yy, 1).wait_recv()

        keys = kv_all[y_rows(yy), :HEAD]
        scores = dot_nt(keys, q_all[...]) * factor
        kpos = (yy * nz + z) * slab + kofs
        scores = jnp.where(kpos <= qpos, scores, masked_score)
        s_all[y_rows(yy), :] = scores
        return jnp.maximum(largest, jnp.max(scores, axis=0, keepdims=True))

    largest = lax.fori_loop(0, y + 1, score_turn, jnp.full((1, nq), masked_score, F32))

    def weight_turn(yy, carry):
        total, mixed = carry
        weights = jnp.exp(s_all[y_rows(yy), :] - largest)
        total = total + jnp.sum(weights, axis=0, keepdims=True)
        mixed = mixed + dot_tn(kv_all[y_rows(yy), HEAD:], weights.astype(BF))
        return total, mixed

    total, mixed = lax.fori_loop(
        0, y + 1, weight_turn, (jnp.zeros((1, nq), F32), jnp.zeros((HEAD, nq), F32))
    )
    for zz in range(nz):
        lanes = slice(zz * HEAD, (zz + 1) * HEAD)
        o_snd[zz] = mixed[:, lanes].astype(BF)
        st_snd[zz, 0:1, :] = largest[:, lanes]
        st_snd[zz, 1:2, :] = total[:, lanes]
    for d in order:
        z_give(1, o_snd, o_rcv, d).start()
        z_give(2, st_snd, st_rcv, d).start()
    o_rcv[z] = o_snd[z]
    st_rcv[z] = st_snd[z]

    for h, p in enumerate(cols):
        remote(upr.at[p], upr.at[p], cs.at[1, h], cr.at[1, h], to_cols[h]).wait_recv()
    up = (upr[0] + upr[1] + upr[2] + upr[3]).astype(BF)
    u_all[z_rows(z), :] = up
    for d in order:
        z_gather(3, u_all, d).start()
    up_t = up.astype(F32).T

    for d in order:
        z_give_arrival(2, st_rcv, d).wait_recv()
        z_give_arrival(1, o_rcv, d).wait_recv()
    top = st_rcv[0, 0:1, :]
    for zz in range(1, nz):
        top = jnp.maximum(top, st_rcv[zz, 0:1, :])
    full_total = jnp.zeros((1, HEAD), F32)
    full = jnp.zeros((HEAD, HEAD), F32)
    for zz in range(nz):
        scale = jnp.exp(st_rcv[zz, 0:1, :] - top)
        full_total = full_total + scale * st_rcv[zz, 1:2, :]
        full = full + scale * o_rcv[zz].astype(F32)
    att_t = (full / full_total).astype(BF).astype(F32)
    ld_snd[0:1, :] = top + jnp.log(full_total)
    ld_snd[1:2, :] = jnp.sum(up_t * att_t, axis=0, keepdims=True)
    ld_rcv[z] = ld_snd[...]

    def ld_copy(d):
        return remote(ld_snd, ld_rcv.at[z], zs.at[4, d], zr.at[4, d], dev_z(d))

    for d in order:
        ld_copy(d).start()
    att_all[c] = att_t.T.astype(BF)
    att_copies = []
    for h, p in enumerate(cols):
        copy = remote(att_all.at[c], att_all.at[c], cs.at[2, h], cr.at[2, h], to_cols[h])
        copy.start()
        att_copies.append(copy)

    for d in order:
        z_gather_arrival(3, u_all, d).wait_recv()
        z_give_arrival(4, ld_rcv, d).wait_recv()
    logsum = jnp.concatenate([ld_rcv[zz, 0:1, :] for zz in range(nz)], axis=1)
    delta = jnp.concatenate([ld_rcv[zz, 1:2, :] for zz in range(nz)], axis=1)

    def dkv_send(yy):
        return remote(
            dkv_snd.at[y_rows(yy)], dkv_rcv.at[y_rows(y)], ds.at[yy], dr.at[y], dev_y(yy)
        )

    def grad_turn(yy, dq):
        keys, values = kv_all[y_rows(yy), :HEAD], kv_all[y_rows(yy), HEAD:]
        probs = jnp.exp(s_all[y_rows(yy), :] - logsum)
        prob_grad = dot_nt(values, u_all[...])
        score_grad = (probs * (prob_grad - delta)).astype(BF)
        dk = jnp.dot(score_grad, q_all[...], preferred_element_type=F32) * factor
        dv = jnp.dot(probs.astype(BF), u_all[...], preferred_element_type=F32)
        dkv_own[:, :HEAD] = dk
        dkv_own[:, HEAD:] = dv

        @pl.when(yy < y)
        def _():
            dkv_snd[y_rows(yy), :] = dkv_own[...].astype(BF)
            dkv_send(yy).start()

        return dq + dot_tn(keys, score_grad)

    dq = lax.fori_loop(0, y + 1, grad_turn, jnp.zeros((HEAD, nq), F32))
    for zz in range(nz):
        dq_snd[zz] = (dq[:, zz * HEAD : (zz + 1) * HEAD] * factor).astype(BF)
    for d in order:
        z_give(5, dq_snd, dq_rcv, d).start()

    for h, p in enumerate(cols):
        remote(att_all.at[p], att_all.at[p], cs.at[2, h], cr.at[2, h], to_cols[h]).wait_recv()
    for j in range(NJ):
        lanes = pl.ds(j * part, part)
        total_out = jnp.dot(att_all[0], wo_v[0, :, lanes], preferred_element_type=F32)
        for p in range(1, 4):
            total_out = total_out + jnp.dot(
                att_all[p], wo_v[p, :, lanes], preferred_element_type=F32
            )
        out_ref[:, lanes] = total_out.astype(BF)

    for d in range(1, ny):

        @pl.when(y + d < ny)
        def _():
            yy = lax.rem(y + d, ny)
            remote(
                dkv_rcv.at[y_rows(yy)], dkv_rcv.at[y_rows(yy)], ds.at[0], dr.at[yy], to_row
            ).wait_recv()
            dkv_own[...] += dkv_rcv[y_rows(yy), :].astype(F32)

    mine = pl.ds(pl.multiple_of(r * HEAD, HEAD), HEAD)
    theirs = pl.ds(pl.multiple_of((1 - r) * HEAD, HEAD), HEAD)
    row_snd[...] = dkv_own[theirs, :].astype(BF)
    row_copy = remote(row_snd, row_rcv, ds.at[ny], dr.at[ny], to_row)
    row_copy.start()
    dq_sum = dq_snd[z].astype(F32)
    for d in order:
        z_give_arrival(5, dq_rcv, d).wait_recv()
        dq_sum = dq_sum + dq_rcv[at_z(-d)].astype(F32)
    dp_all[c, mine, :HEAD] = dq_sum.T.astype(BF)
    row_copy.wait_recv()
    dp_all[c, mine, HEAD:] = (dkv_own[mine, :] + row_rcv[...].astype(F32)).astype(BF)

    peers = [(r, across), (1 - r, c), (1 - r, across)]

    def dp_rows(rr):
        return pl.ds(pl.multiple_of(rr * HEAD, HEAD), HEAD)

    def dp_copy(i):
        src = dp_all.at[c, mine]
        dev = to_cols[0] if i == 3 else (s,) + peers[i]
        return remote(src, src, gs.at[i], gr.at[i], dev)

    def dp_relay(i):
        rr, cc = peers[i]
        src = dp_all.at[cc, dp_rows(rr)]
        return remote(src, src, gs.at[4 + i], gr.at[4 + i], to_cols[0])

    def dp_arrival(i):
        if i == 3:
            rr, cc = r, sibling
        elif i < 3:
            rr, cc = peers[i]
        else:
            rr, cc = ((r, far), (1 - r, sibling), (1 - r, far))[i - 4]
        src = dp_all.at[cc, dp_rows(rr)]
        return remote(src, src, gs.at[i], gr.at[i], to_cols[0])

    for i in (2, 0, 1, 3):
        dp_copy(i).start()
    for i in (0, 1, 2):
        dp_arrival(i).wait_recv()
        dp_relay(i).start()
    for i in range(3, 7):
        dp_arrival(i).wait_recv()
    dp_ref[...] = dp_all[...]

    kv_row().wait_send()
    for d in range(1, ny):

        @pl.when(y + d < ny)
        def _():
            kv_send(d, 0).wait_send()
            kv_send(d, 1).wait_send()

    def sent_turn(yy, carry):
        dkv_send(yy).wait_send()
        return carry

    lax.fori_loop(0, y, sent_turn, 0)
    for d in order:
        z_gather(0, q_all, d).wait_send()
        z_give(1, o_snd, o_rcv, d).wait_send()
        z_give(2, st_snd, st_rcv, d).wait_send()
        z_gather(3, u_all, d).wait_send()
        ld_copy(d).wait_send()
        z_give(5, dq_snd, dq_rcv, d).wait_send()
    wo_sib.wait_send()
    row_copy.wait_send()
    for copy in ups_copies + att_copies:
        copy.wait_send()
    for i in range(4):
        dp_copy(i).wait_send()
    for i in range(3):
        dp_relay(i).wait_send()


def attention(ny, nz, packed, cotangent, wo, wo_other):
    width = cotangent.shape[1]
    hbm = pl.BlockSpec(memory_space=pl.ANY)
    vm = pl.BlockSpec(memory_space=pltpu.VMEM)
    nk, nq = ny * 2 * HEAD, nz * HEAD
    n = packed.shape[1]
    V = pltpu.VMEM
    sem = pltpu.SemaphoreType.DMA
    return pl.pallas_call(
        functools.partial(attention_kernel, ny, nz),
        out_shape=(
            jax.ShapeDtypeStruct(cotangent.shape, BF),
            jax.ShapeDtypeStruct((4, 2 * HEAD, n), BF),
        ),
        in_specs=[vm, hbm, hbm, hbm],
        out_specs=(vm, vm),
        scratch_shapes=[
            V((nq, HEAD), BF),
            V((nk, 2 * HEAD), BF),
            V((nq, HEAD), BF),
            V((HEAD, width), BF),
            V((4, HEAD, width), BF),
            V((4, HEAD, HEAD), F32),
            V((4, HEAD, HEAD), F32),
            V((nk, nq), F32),
            V((nz, HEAD, HEAD), BF),
            V((nz, HEAD, HEAD), BF),
            V((nz, 8, HEAD), F32),
            V((nz, 8, HEAD), F32),
            V((8, HEAD), F32),
            V((nz, 8, HEAD), F32),
            V((4, HEAD, HEAD), BF),
            V((HEAD, nq), F32),
            V((nz, HEAD, HEAD), BF),
            V((nz, HEAD, HEAD), BF),
            V((2 * HEAD, 2 * HEAD), F32),
            V((nk, 2 * HEAD), BF),
            V((nk, 2 * HEAD), BF),
            V((HEAD, 2 * HEAD), BF),
            V((HEAD, 2 * HEAD), BF),
            V((4, 2 * HEAD, n), BF),
            sem((2 + 2 * NJ,)),
            sem((6, nz)),
            sem((6, nz)),
            sem((1 + 2 * ny + 2,)),
            sem((2 * ny + 1,)),
            sem((3, 3)),
            sem((3, 3)),
            sem((ny + 1,)),
            sem((ny + 1,)),
            sem((7,)),
            sem((7,)),
        ],
        compiler_params=pltpu.CompilerParams(
            collective_id=2, has_side_effects=True, vmem_limit_bytes=48 * 2**20
        ),
        cost_estimate=pl.CostEstimate(
            flops=3_000_000_000, bytes_accessed=120_000_000, transcendentals=2_000_000
        ),
        name="attention",
    )(packed, cotangent, wo, wo_other)


def input_grad_kernel(c_ref, dp_ref, own_ref, sib_ref, oth_ref, out_ref):
    c = c_ref[0]
    n = own_ref.shape[1]
    acc = dot_nt(dp_ref[c], own_ref[...])
    acc = acc + dot_nt(dp_ref[flip(c, 1)], sib_ref[...])
    acc = acc + dot_nt(dp_ref[flip(c, 2)], oth_ref[:, :n])
    acc = acc + dot_nt(dp_ref[flip(c, 3)], oth_ref[:, n:])
    out_ref[...] = acc.astype(BF)


def input_grad(dp, w, w_sib, w_other):
    depth, n = w_sib.shape
    rows = dp.shape[1]
    blk = min(256, depth)
    steps = depth // blk
    c = lax.axis_index("col").astype(jnp.int32).reshape(1)
    return pl.pallas_call(
        input_grad_kernel,
        out_shape=jax.ShapeDtypeStruct((rows, depth), BF),
        grid_spec=pltpu.PrefetchScalarGridSpec(
            num_scalar_prefetch=1,
            grid=(steps,),
            in_specs=[
                pl.BlockSpec(dp.shape, lambda i, c: (0, 0, 0)),
                pl.BlockSpec((blk, n), lambda i, c: (c[0] * steps + i, 0)),
                pl.BlockSpec((blk, n), lambda i, c: (i, 0)),
                pl.BlockSpec((blk, 2 * n), lambda i, c: (i, 0)),
            ],
            out_specs=pl.BlockSpec((rows, blk), lambda i, c: (0, i)),
        ),
        name="input_grad",
    )(c, dp, w, w_sib, w_other)


def body(nz, tokens, input_weight, output_weight, output_cotangent):
    ny = lax.axis_size("seq") // nz
    seed_w, seed_wo = seeds(input_weight, output_weight)
    wo_other = lax.all_gather(seed_wo, "seq", axis=0, tiled=True)
    w_other = lax.all_gather(seed_w, "seq", axis=0, tiled=True)
    packed, w_sib = project(tokens, input_weight)
    layer_output, dp = attention(
        ny, nz, packed, output_cotangent, output_weight, wo_other
    )
    return layer_output, input_grad(dp, input_weight, w_sib, w_other)


def solution(mesh):
    nz = 8 if mesh.shape["seq"] % 32 == 0 else 2
    return jax.shard_map(
        functools.partial(body, nz),
        mesh=mesh,
        in_specs=(
            P("seq", ("row", "col")),
            P("row", "col"),
            P("col", None),
            P(("seq", "row"), "col"),
        ),
        out_specs=(P(("seq", "row"), "col"), P("seq", ("row", "col"))),
        check_vma=False,
    )
```

```python
import functools
import math

import jax
import jax.numpy as jnp
from jax import lax
from jax.experimental import pallas as pl
from jax.experimental.pallas import tpu as pltpu
from jax.sharding import PartitionSpec as P

HEAD = 128
MESH = pl.DeviceIdType.MESH
masked_score = -1e30
BF = jnp.bfloat16
F32 = jnp.float32
CHUNKS = 4


def remote(src, dst, send_sem, recv_sem, device):
    return pltpu.make_async_remote_copy(
        src_ref=src,
        dst_ref=dst,
        send_sem=send_sem,
        recv_sem=recv_sem,
        device_id=device,
        device_id_type=MESH,
    )


def greet(devices):
    barrier = pltpu.get_barrier_semaphore()
    for device in devices:
        pl.semaphore_signal(barrier, inc=1, device_id=device, device_id_type=MESH)
    pl.semaphore_wait(barrier, len(devices))


def dot_nt(a, b):
    return lax.dot_general(a, b, (((1,), (1,)), ((), ())), preferred_element_type=F32)


def dot_tn(a, b):
    return lax.dot_general(a, b, (((0,), (0,)), ((), ())), preferred_element_type=F32)


def flip(c, bits):
    low, high = lax.rem(c, 2), c // 2
    if bits & 1:
        low = 1 - low
    if bits & 2:
        high = 1 - high
    return high * 2 + low


def ring(size):
    return size // 2, (size - 1) // 2


def layer_kernel(
    ny,
    nz,
    t_ref,
    w_ref,
    wo_ref,
    do_ref,
    out_ref,
    dx_ref,
    tbuf,
    wv,
    psend,
    precv,
    w_x,
    wo_v,
    q_all,
    kv_all,
    u_all,
    do_v,
    ups,
    upr,
    s_all,
    o_snd,
    o_rcv,
    st_snd,
    st_rcv,
    ld_snd,
    ld_rcv,
    att_all,
    dq_snd,
    dq_rcv,
    dkv_own,
    dkv_snd,
    dkv_rcv,
    row_snd,
    row_rcv,
    dp_all,
    lsem,
    sds,
    sdr,
    wzs,
    wzr,
    wys,
    wyr,
    oys,
    oyr,
    ozs,
    ozr,
    sbs,
    sbr,
    tks,
    tkr,
    pts,
    ptr,
    zs,
    zr,
    kvs,
    kvr,
    cs,
    cr,
    ds,
    dr,
    gs,
    gr,
):
    s, r, c = lax.axis_index("seq"), lax.axis_index("row"), lax.axis_index("col")
    y, z = s // nz, lax.rem(s, nz)
    core = lax.rem(c, 2)
    sgn = 1 - 2 * core
    factor = 1.0 / math.sqrt(HEAD)
    depth = t_ref.shape[1]
    width = do_ref.shape[1]
    step = 2 * HEAD // CHUNKS
    hk = CHUNKS // 2
    slab = 2 * HEAD
    cols = [c, flip(c, 1), flip(c, 2), flip(c, 3)]
    to_cols = [(s, r, p) for p in cols]
    to_row = (s, 1 - r, c)
    to_diag = (s, 1 - r, cols[2])

    def wrap(a, n):
        return lax.rem(a + 2 * n, n)

    def dev_z(zz):
        return (y * nz + zz, r, c)

    def dev_y(yy):
        return (yy * nz + z, r, c)

    own_tokens = pltpu.make_async_copy(t_ref, tbuf.at[0], lsem.at[0])
    own_w = pltpu.make_async_copy(w_ref, wv, lsem.at[1])
    own_wo = pltpu.make_async_copy(
        wo_ref.at[:, pl.ds(pl.multiple_of(c * width, 128), width)], wo_v.at[0], lsem.at[2]
    )
    own_do = pltpu.make_async_copy(do_ref, do_v, lsem.at[3])
    own_tokens.start()
    own_w.start()
    own_wo.start()
    own_do.start()
    greet(
        [dev_z(wrap(z + d, nz)) for d in range(1, nz)]
        + [dev_y(wrap(y + d, ny)) for d in range(1, ny)]
        + [to_row]
        + to_cols[1:]
        + [to_diag]
    )

    piece = depth // (ny * nz)
    orow = HEAD // nz
    part = width // ny

    def w_piece(yy, zz):
        start = pl.multiple_of((yy * nz + zz) * piece, 16)
        return w_x.at[pl.ds(1, 2), pl.ds(start, piece), :]

    def o_piece(yy, zz):
        return wo_v.at[
            pl.ds(2, 2),
            pl.ds(pl.multiple_of(zz * orow, 16), orow),
            pl.ds(pl.multiple_of(yy * part, 128), part),
        ]

    def o_super(zz):
        return wo_v.at[pl.ds(2, 2), pl.ds(pl.multiple_of(zz * orow, 16), orow), :]

    seeds = []
    for h in range(2):
        p = cols[2 + h]
        start = pl.multiple_of(s * piece, 16)
        seeds.append(
            remote(
                w_ref.at[pl.ds(pl.multiple_of(p * depth + s * piece, 16), piece), :],
                w_x.at[1 + h, pl.ds(start, piece), :],
                sds.at[0, h],
                sdr.at[0, h],
                to_cols[2 + h],
            )
        )
        orows = pl.ds(pl.multiple_of(z * orow, 16), orow)
        seeds.append(
            remote(
                wo_ref.at[orows, pl.ds(pl.multiple_of(p * width + y * part, 128), part)],
                wo_v.at[2 + h, orows, pl.ds(pl.multiple_of(y * part, 128), part)],
                sds.at[1, h],
                sdr.at[1, h],
                to_cols[2 + h],
            )
        )
    for copy in seeds:
        copy.start()

    def rows_of(k):
        start = (1 - r) * HEAD + k * step if k < hk else r * HEAD + (k - hk) * step
        return pl.ds(pl.multiple_of(start, step), step)

    def token_copy(kind, k):
        rows = rows_of(k)
        if kind == 0:
            return remote(
                t_ref.at[rows], tbuf.at[2, rows], tks.at[0, k], tkr.at[0, k], to_cols[2]
            )
        if kind == 1:
            return remote(
                t_ref.at[rows], tbuf.at[1, rows], tks.at[1, k], tkr.at[1, k], to_cols[1]
            )
        return remote(
            tbuf.at[2, rows], tbuf.at[3, rows], tks.at[2, k], tkr.at[2, k], to_cols[1]
        )

    for k in range(CHUNKS):
        token_copy(0, k).start()
        token_copy(1, k).start()

    sib_w = remote(
        w_ref.at[pl.ds(pl.multiple_of(cols[1] * depth, 16), depth), :],
        w_x.at[0],
        sbs.at[0],
        sbr.at[0],
        to_cols[1],
    )
    sib_wo = remote(
        wo_ref.at[:, pl.ds(pl.multiple_of(cols[1] * width, 128), width)],
        wo_v.at[1],
        sbs.at[1],
        sbr.at[1],
        to_cols[1],
    )
    sib_wo.start()
    sib_w.start()

    zl, zsh = ring(nz)
    yl, ysh = ring(ny)
    z_next, z_prev = wrap(z + sgn, nz), wrap(z - sgn, nz)
    y_next, y_prev = wrap(y + sgn, ny), wrap(y - sgn, ny)

    def zq(long, t):
        return wrap(z - sgn * t, nz) if long else wrap(z + sgn * t, nz)

    def yq(long, t):
        return wrap(y - sgn * t, ny) if long else wrap(y + sgn * t, ny)

    def z_ring(pick, snd, rcv, long, t):
        ref = pick(zq(long, t))
        way = 0 if long else 1
        return remote(
            ref, ref, snd.at[way, t], rcv.at[way, t + 1], dev_z(z_next if long else z_prev)
        )

    def z_ring_in(pick, snd, rcv, long, t):
        ref = pick(zq(long, t))
        way = 0 if long else 1
        return remote(ref, ref, snd.at[way, t], rcv.at[way, t], dev_z(z_next))

    def y_ring(pick, snd, rcv, long, t):
        ref = pick(yq(long, t))
        way = 0 if long else 1
        return remote(
            ref, ref, snd.at[way, t], rcv.at[way, t + 1], dev_y(y_next if long else y_prev)
        )

    def y_ring_in(pick, snd, rcv, long, t):
        ref = pick(yq(long, t))
        way = 0 if long else 1
        return remote(ref, ref, snd.at[way, t], rcv.at[way, t], dev_y(y_next))

    started = []

    def go(copy):
        copy.start()
        started.append(copy)

    def w_here(zz):
        return w_piece(y, zz)

    def o_here(yy):
        return o_piece(yy, z)

    def z_start(pick, snd, rcv):
        if zl:
            go(z_ring(pick, snd, rcv, True, 0))
        if zsh:
            go(z_ring(pick, snd, rcv, False, 0))

    def y_start(pick, snd, rcv):
        if yl:
            go(y_ring(pick, snd, rcv, True, 0))
        if ysh:
            go(y_ring(pick, snd, rcv, False, 0))

    def z_round(pick, snd, rcv, t):
        ways = []
        for long, hops in ((True, zl), (False, zsh)):
            if t <= hops:
                z_ring_in(pick, snd, rcv, long, t).wait_recv()
                if t < hops:
                    go(z_ring(pick, snd, rcv, long, t))
                ways.append(long)
        return ways

    def y_round(pick, snd, rcv, t):
        for long, hops in ((True, yl), (False, ysh)):
            if t <= hops:
                y_ring_in(pick, snd, rcv, long, t).wait_recv()
                if t < hops:
                    go(y_ring(pick, snd, rcv, long, t))

    def w_column(long, t):
        zz = zq(long, t)
        index = t if long else zl + t

        def pick(yy):
            return w_piece(yy, zz)

        return pick, wys.at[index], wyr.at[index]

    def product(i, rows, start):
        return jnp.dot(
            tbuf[i, rows, :],
            wv[pl.ds(pl.multiple_of(start, 16), depth), :],
            preferred_element_type=F32,
        )

    def part_copy(k):
        rows = pl.ds(k * step, step)
        return remote(psend.at[rows], precv.at[rows], pts.at[k], ptr.at[k], to_row)

    def z_rows(zz):
        return pl.ds(pl.multiple_of(zz * HEAD, HEAD), HEAD)

    def kv_rows(yy, rr):
        return pl.ds(pl.multiple_of(yy * slab + rr * HEAD, HEAD), HEAD)

    def project(k):
        rows = rows_of(k)

        def arrived(kind):
            ref = tbuf.at[(2, 1, 3)[kind], rows]
            remote(ref, ref, tks.at[kind, k], tkr.at[kind, k], to_cols[1]).wait_recv()

        arrived(0)
        go(token_copy(2, k))
        arrived(1)
        acc = product(0, rows, c * depth) + product(1, rows, cols[1] * depth)
        acc = acc + product(2, rows, cols[2] * depth)
        arrived(2)
        acc = acc + product(3, rows, cols[3] * depth)
        if k < hk:
            psend[pl.ds(k * step, step), :] = acc
            go(part_copy(k))
        else:
            part_copy(k - hk).wait_recv()
            out = pl.ds((k - hk) * step, step)
            packed = (acc + precv[out, :]).astype(BF)
            q_all[pl.ds(pl.multiple_of(z * HEAD + (k - hk) * step, step), step), :] = packed[
                :, :HEAD
            ]
            start = pl.multiple_of(y * slab + r * HEAD + (k - hk) * step, step)
            kv_all[pl.ds(start, step), :] = packed[:, HEAD:]

    for copy in seeds:
        copy.wait_recv()
    z_start(w_here, wzs, wzr)
    y_start(o_here, oys, oyr)
    pick, snd, rcv = w_column(True, 0)
    y_start(pick, snd, rcv)
    columns = [[(True, 0)]]
    own_tokens.wait()
    own_w.wait()
    for t in range(1, yl + 1):
        y_round(o_here, oys, oyr, t)
    z_start(o_super, ozs, ozr)
    for k in range(max(CHUNKS, zl)):
        t = k + 1
        if k < CHUNKS:
            project(k)
        if t <= zl:
            ways = z_round(w_here, wzs, wzr, t)
            for long in ways:
                y_start(*w_column(long, t))
            columns.append([(long, t) for long in ways])
            for column in columns[t - 1]:
                y_round(*w_column(*column), 1)
            z_round(o_super, ozs, ozr, t)

    def kv_row():
        rows = kv_rows(y, r)
        return remote(kv_all.at[rows], kv_all.at[rows], kvs.at[0], kvr.at[2 * ny], to_row)

    def kv_row_arrival():
        rows = kv_rows(y, 1 - r)
        return remote(kv_all.at[rows], kv_all.at[rows], kvs.at[0], kvr.at[2 * ny], to_row)

    def kv_send(d, other):
        rr = 1 - r if other else r
        rows = kv_rows(y, rr)
        return remote(
            kv_all.at[rows],
            kv_all.at[rows],
            kvs.at[1 + 2 * d + other],
            kvr.at[2 * y + other],
            dev_y(wrap(y + d, ny)),
        )

    def kv_arrival(yy, other):
        rr = 1 - r if other else r
        rows = kv_rows(yy, rr)
        return remote(kv_all.at[rows], kv_all.at[rows], kvs.at[0], kvr.at[2 * yy + other], to_row)

    go(kv_row())
    for d in range(1, ny):

        @pl.when(y + d < ny)
        def _():
            kv_send(d, 0).start()

    def z_gather(kind, buf, d):
        return remote(
            buf.at[z_rows(z)],
            buf.at[z_rows(z)],
            zs.at[kind, d],
            zr.at[kind, d],
            dev_z(wrap(z + d, nz)),
        )

    def z_gather_arrival(kind, buf, d):
        rows = z_rows(wrap(z - d, nz))
        return remote(buf.at[rows], buf.at[rows], zs.at[kind, d], zr.at[kind, d], dev_z(z_next))

    def z_give(kind, src, dst, d):
        to = wrap(z + d, nz)
        return remote(src.at[to], dst.at[z], zs.at[kind, d], zr.at[kind, d], dev_z(to))

    def z_give_arrival(kind, dst, d):
        slot = wrap(z - d, nz)
        return remote(dst.at[slot], dst.at[slot], zs.at[kind, d], zr.at[kind, d], dev_z(z_next))

    order = sorted(range(1, nz), key=lambda d: -min(d, nz - d))
    for d in order:
        go(z_gather(0, q_all, d))

    for column in columns[zl]:
        y_round(*w_column(*column), 1)

    kv_row_arrival().wait_recv()
    for d in range(1, ny):

        @pl.when(y + d < ny)
        def _():
            kv_send(d, 1).start()

    own_do.wait()
    own_wo.wait()
    sib_wo.wait_recv()
    for i in range(1, 4):
        ups[i] = dot_nt(do_v[...], wo_v[i])
        go(remote(ups.at[i], upr.at[i], cs.at[0, i], cr.at[0, i], to_cols[i]))
    upr[0] = dot_nt(do_v[...], wo_v[0])

    for d in order:
        z_gather_arrival(0, q_all, d).wait_recv()
    nq = nz * HEAD
    lane = lax.broadcasted_iota(jnp.int32, (1, nq), 1)
    qpos = (y * nz + lane // HEAD) * slab + r * HEAD + lane % HEAD
    kofs = lax.broadcasted_iota(jnp.int32, (slab, 1), 0)

    def y_rows(yy):
        return pl.ds(pl.multiple_of(yy * slab, slab), slab)

    def score_turn(yy, largest):
        @pl.when(yy < y)
        def _():
            kv_arrival(yy, 0).wait_recv()
            kv_arrival(yy, 1).wait_recv()

        keys = kv_all[y_rows(yy), :HEAD]
        scores = dot_nt(keys, q_all[...]) * factor
        kpos = (yy * nz + z) * slab + kofs
        scores = jnp.where(kpos <= qpos, scores, masked_score)
        s_all[y_rows(yy), :] = scores
        return jnp.maximum(largest, jnp.max(scores, axis=0, keepdims=True))

    largest = lax.fori_loop(0, y + 1, score_turn, jnp.full((1, nq), masked_score, F32))

    def weight_turn(yy, carry):
        total, mixed = carry
        weights = jnp.exp(s_all[y_rows(yy), :] - largest)
        total = total + jnp.sum(weights, axis=0, keepdims=True)
        mixed = mixed + dot_tn(kv_all[y_rows(yy), HEAD:], weights.astype(BF))
        return total, mixed

    total, mixed = lax.fori_loop(
        0, y + 1, weight_turn, (jnp.zeros((1, nq), F32), jnp.zeros((HEAD, nq), F32))
    )
    for zz in range(nz):
        lanes = slice(zz * HEAD, (zz + 1) * HEAD)
        o_snd[zz] = mixed[:, lanes].astype(BF)
        st_snd[zz, 0:1, :] = largest[:, lanes]
        st_snd[zz, 1:2, :] = total[:, lanes]
    for d in order:
        go(z_give(1, o_snd, o_rcv, d))
        go(z_give(2, st_snd, st_rcv, d))
    o_rcv[z] = o_snd[z]
    st_rcv[z] = st_snd[z]

    for i in range(1, 4):
        remote(upr.at[i], upr.at[i], cs.at[0, i], cr.at[0, i], to_cols[i]).wait_recv()
    up = (upr[0] + upr[1] + upr[2] + upr[3]).astype(BF)
    u_all[z_rows(z), :] = up
    for d in order:
        go(z_gather(3, u_all, d))
    up_t = up.astype(F32).T

    for d in order:
        z_give_arrival(2, st_rcv, d).wait_recv()
        z_give_arrival(1, o_rcv, d).wait_recv()
    top = st_rcv[0, 0:1, :]
    for zz in range(1, nz):
        top = jnp.maximum(top, st_rcv[zz, 0:1, :])
    full_total = jnp.zeros((1, HEAD), F32)
    full = jnp.zeros((HEAD, HEAD), F32)
    for zz in range(nz):
        scale = jnp.exp(st_rcv[zz, 0:1, :] - top)
        full_total = full_total + scale * st_rcv[zz, 1:2, :]
        full = full + scale * o_rcv[zz].astype(F32)
    att_t = (full / full_total).astype(BF).astype(F32)
    ld_snd[0:1, :] = top + jnp.log(full_total)
    ld_snd[1:2, :] = jnp.sum(up_t * att_t, axis=0, keepdims=True)
    ld_rcv[z] = ld_snd[...]
    for d in order:
        go(remote(ld_snd, ld_rcv.at[z], zs.at[4, d], zr.at[4, d], dev_z(wrap(z + d, nz))))
    att_all[0] = att_t.T.astype(BF)
    for i in range(1, 4):
        go(remote(att_all.at[0], att_all.at[i], cs.at[1, i], cr.at[1, i], to_cols[i]))

    for d in order:
        z_gather_arrival(3, u_all, d).wait_recv()
        z_give_arrival(4, ld_rcv, d).wait_recv()
    logsum = jnp.concatenate([ld_rcv[zz, 0:1, :] for zz in range(nz)], axis=1)
    delta = jnp.concatenate([ld_rcv[zz, 1:2, :] for zz in range(nz)], axis=1)

    def dkv_send(yy):
        return remote(
            dkv_snd.at[y_rows(yy)], dkv_rcv.at[y_rows(y)], ds.at[yy], dr.at[y], dev_y(yy)
        )

    def grad_turn(yy, dq):
        keys, values = kv_all[y_rows(yy), :HEAD], kv_all[y_rows(yy), HEAD:]
        probs = jnp.exp(s_all[y_rows(yy), :] - logsum)
        prob_grad = dot_nt(values, u_all[...])
        score_grad = (probs * (prob_grad - delta)).astype(BF)
        dk = jnp.dot(score_grad, q_all[...], preferred_element_type=F32) * factor
        dv = jnp.dot(probs.astype(BF), u_all[...], preferred_element_type=F32)
        dkv_own[:, :HEAD] = dk
        dkv_own[:, HEAD:] = dv

        @pl.when(yy < y)
        def _():
            dkv_snd[y_rows(yy), :] = dkv_own[...].astype(BF)
            dkv_send(yy).start()

        return dq + dot_tn(keys, score_grad)

    dq = lax.fori_loop(0, y + 1, grad_turn, jnp.zeros((HEAD, nq), F32))
    for zz in range(nz):
        dq_snd[zz] = (dq[:, zz * HEAD : (zz + 1) * HEAD] * factor).astype(BF)
    for d in order:
        go(z_give(5, dq_snd, dq_rcv, d))

    for i in range(1, 4):
        remote(att_all.at[i], att_all.at[i], cs.at[1, i], cr.at[1, i], to_cols[i]).wait_recv()
    for j in range(ny):
        lanes = pl.ds(j * part, part)
        total_out = jnp.dot(att_all[0], wo_v[0, :, lanes], preferred_element_type=F32)
        for i in range(1, 4):
            total_out = total_out + jnp.dot(
                att_all[i], wo_v[i, :, lanes], preferred_element_type=F32
            )
        out_ref[:, lanes] = total_out.astype(BF)

    for d in range(1, ny):

        @pl.when(y + d < ny)
        def _():
            yy = wrap(y + d, ny)
            ref = dkv_rcv.at[y_rows(yy)]
            remote(ref, ref, ds.at[0], dr.at[yy], to_row).wait_recv()
            dkv_own[...] += dkv_rcv[y_rows(yy), :].astype(F32)

    def dp_rows(rr):
        return pl.ds(pl.multiple_of(rr * HEAD, HEAD), HEAD)

    mine, theirs = dp_rows(r), dp_rows(1 - r)
    row_snd[...] = dkv_own[theirs, :].astype(BF)
    row_copy = remote(row_snd, row_rcv, ds.at[ny], dr.at[ny], to_row)
    go(row_copy)
    dq_sum = dq_snd[z].astype(F32)
    for d in order:
        z_give_arrival(5, dq_rcv, d).wait_recv()
        dq_sum = dq_sum + dq_rcv[wrap(z - d, nz)].astype(F32)
    dp_all[0, mine, :HEAD] = dq_sum.T.astype(BF)
    row_copy.wait_recv()
    dp_all[0, mine, HEAD:] = (dkv_own[mine, :] + row_rcv[...].astype(F32)).astype(BF)

    peers = [to_cols[2], to_row, to_diag]
    slots = [(2, r), (0, 1 - r), (2, 1 - r)]

    def dp_copy(i):
        dst = dp_all.at[(2, 0, 2, 1)[i], mine]
        return remote(
            dp_all.at[0, mine], dst, gs.at[i], gr.at[i], to_cols[1] if i == 3 else peers[i]
        )

    def dp_relay(i):
        col, rr = slots[i]
        return remote(
            dp_all.at[col, dp_rows(rr)],
            dp_all.at[col + 1, dp_rows(rr)],
            gs.at[4 + i],
            gr.at[4 + i],
            to_cols[1],
        )

    def dp_arrival(i):
        col, rr = (1, r) if i == 3 else slots[i % 4]
        col = col + 1 if i > 3 else col
        ref = dp_all.at[col, dp_rows(rr)]
        remote(ref, ref, gs.at[i], gr.at[i], to_cols[1]).wait_recv()

    for i in (2, 1, 0, 3):
        go(dp_copy(i))

    for t in range(2, yl + 1):
        for round_columns in columns:
            for column in round_columns:
                y_round(*w_column(*column), t)
    sib_w.wait_recv()

    def dx_half(rr):
        rows = dp_rows(rr)
        blk = min(256, depth)

        def turn(j, carry):
            start = pl.multiple_of(j * blk, blk)
            acc = dot_nt(dp_all[0, rows, :], wv[pl.ds(c * depth + start, blk), :])
            for i in range(1, 4):
                acc = acc + dot_nt(dp_all[i, rows, :], w_x[i - 1, pl.ds(start, blk), :])
            dx_ref[rows, pl.ds(start, blk)] = acc.astype(BF)
            return carry

        lax.fori_loop(0, depth // blk, turn, 0)

    dp_arrival(0)
    go(dp_relay(0))
    dp_arrival(1)
    go(dp_relay(1))
    dp_arrival(2)
    go(dp_relay(2))
    dp_arrival(3)
    dp_arrival(4)
    dx_half(r)
    dp_arrival(5)
    dp_arrival(6)
    dx_half(1 - r)

    for d in range(1, ny):

        @pl.when(y + d < ny)
        def _():
            kv_send(d, 0).wait_send()
            kv_send(d, 1).wait_send()

    def sent_turn(yy, carry):
        dkv_send(yy).wait_send()
        return carry

    lax.fori_loop(0, y, sent_turn, 0)
    for copy in seeds + [sib_w, sib_wo] + started:
        copy.wait_send()
    for k in range(CHUNKS):
        token_copy(0, k).wait_send()
        token_copy(1, k).wait_send()


def body(nz, tokens, input_weight, output_weight, output_cotangent):
    ny = lax.axis_size("seq") // nz
    rows, depth = tokens.shape
    n = input_weight.shape[1]
    width = output_cotangent.shape[1]
    hbm = pl.BlockSpec(memory_space=pl.ANY)
    vm = pl.BlockSpec(memory_space=pltpu.VMEM)
    nk, nq = ny * 2 * HEAD, nz * HEAD
    V = pltpu.VMEM
    sem = pltpu.SemaphoreType.DMA
    zl, zsh = ring(nz)
    yl, ysh = ring(ny)
    return pl.pallas_call(
        functools.partial(layer_kernel, ny, nz),
        out_shape=(
            jax.ShapeDtypeStruct(output_cotangent.shape, BF),
            jax.ShapeDtypeStruct(tokens.shape, BF),
        ),
        in_specs=[hbm] * 4,
        out_specs=(vm, vm),
        scratch_shapes=[
            V((4, rows, depth), BF),
            V((4 * depth, n), BF),
            V((HEAD, n), F32),
            V((HEAD, n), F32),
            V((3, depth, n), BF),
            V((4, HEAD, width), BF),
            V((nq, HEAD), BF),
            V((nk, 2 * HEAD), BF),
            V((nq, HEAD), BF),
            V((HEAD, width), BF),
            V((4, HEAD, HEAD), F32),
            V((4, HEAD, HEAD), F32),
            V((nk, nq), F32),
            V((nz, HEAD, HEAD), BF),
            V((nz, HEAD, HEAD), BF),
            V((nz, 8, HEAD), F32),
            V((nz, 8, HEAD), F32),
            V((8, HEAD), F32),
            V((nz, 8, HEAD), F32),
            V((4, HEAD, HEAD), BF),
            V((nz, HEAD, HEAD), BF),
            V((nz, HEAD, HEAD), BF),
            V((2 * HEAD, 2 * HEAD), F32),
            V((nk, 2 * HEAD), BF),
            V((nk, 2 * HEAD), BF),
            V((HEAD, 2 * HEAD), BF),
            V((HEAD, 2 * HEAD), BF),
            V((4, 2 * HEAD, n), BF),
            sem((4,)),
            sem((2, 2)),
            sem((2, 2)),
            sem((2, zl + 1)),
            sem((2, zl + 1)),
            sem((nz, 2, yl + 1)),
            sem((nz, 2, yl + 1)),
            sem((2, yl + 1)),
            sem((2, yl + 1)),
            sem((2, zl + 1)),
            sem((2, zl + 1)),
            sem((2,)),
            sem((2,)),
            sem((3, CHUNKS)),
            sem((3, CHUNKS)),
            sem((CHUNKS // 2,)),
            sem((CHUNKS // 2,)),
            sem((6, nz)),
            sem((6, nz)),
            sem((1 + 2 * ny + 2,)),
            sem((2 * ny + 1,)),
            sem((2, 4)),
            sem((2, 4)),
            sem((ny + 1,)),
            sem((ny + 1,)),
            sem((7,)),
            sem((7,)),
        ],
        compiler_params=pltpu.CompilerParams(
            collective_id=0, has_side_effects=True, vmem_limit_bytes=60 * 2**20
        ),
        cost_estimate=pl.CostEstimate(
            flops=6_000_000_000, bytes_accessed=20_000_000, transcendentals=2_000_000
        ),
        name="layer",
    )(tokens, input_weight, output_weight, output_cotangent)


def solution(mesh):
    seq = mesh.shape["seq"]
    nz = 8 if seq % 32 == 0 else seq // 2
    return jax.shard_map(
        functools.partial(body, nz),
        mesh=mesh,
        in_specs=(
            P("seq", ("row", "col")),
            P("row", "col"),
            P("col", None),
            P(("seq", "row"), "col"),
        ),
        out_specs=(P(("seq", "row"), "col"), P("seq", ("row", "col"))),
        check_vma=False,
    )
```

```python
import functools
import math

import jax
import jax.numpy as jnp
from jax import lax
from jax.experimental import pallas as pl
from jax.experimental.pallas import tpu as pltpu
from jax.sharding import PartitionSpec as P

HEAD = 128
MESH = pl.DeviceIdType.MESH
masked_score = -1e30
BF = jnp.bfloat16
F32 = jnp.float32
CHUNKS = 4


def remote(src, dst, send_sem, recv_sem, device):
    return pltpu.make_async_remote_copy(
        src_ref=src,
        dst_ref=dst,
        send_sem=send_sem,
        recv_sem=recv_sem,
        device_id=device,
        device_id_type=MESH,
    )


def greet(devices):
    barrier = pltpu.get_barrier_semaphore()
    for device in devices:
        pl.semaphore_signal(barrier, inc=1, device_id=device, device_id_type=MESH)
    pl.semaphore_wait(barrier, len(devices))


def dot_nt(a, b):
    return lax.dot_general(a, b, (((1,), (1,)), ((), ())), preferred_element_type=F32)


def dot_tn(a, b):
    return lax.dot_general(a, b, (((0,), (0,)), ((), ())), preferred_element_type=F32)


def flip(c, bits):
    low, high = lax.rem(c, 2), c // 2
    if bits & 1:
        low = 1 - low
    if bits & 2:
        high = 1 - high
    return high * 2 + low


def ring(size):
    return size // 2, (size - 1) // 2


def layer_kernel(
    ny,
    nz,
    t_ref,
    w_ref,
    wo_ref,
    do_ref,
    out_ref,
    dx_ref,
    tbuf,
    wv,
    psend,
    precv,
    w_x,
    wo_v,
    q_all,
    kv_all,
    u_all,
    do_v,
    ups,
    upr,
    s_all,
    o_snd,
    o_rcv,
    st_snd,
    st_rcv,
    ld_snd,
    ld_rcv,
    att_all,
    dq_snd,
    dq_rcv,
    dkv_own,
    dkv_snd,
    dkv_rcv,
    dp_all,
    lsem,
    sds,
    sdr,
    wzs,
    wzr,
    wys,
    wyr,
    ozs,
    ozr,
    sbs,
    sbr,
    tks,
    tkr,
    pts,
    ptr,
    qs,
    qr,
    uzs,
    uzr,
    zs,
    zr,
    kvs,
    kvr,
    cs,
    cr,
    ds,
    dr,
    gs,
    gr,
):
    s, r, c = lax.axis_index("seq"), lax.axis_index("row"), lax.axis_index("col")
    y, z = s // nz, lax.rem(s, nz)
    core = lax.rem(c, 2)
    sgn = 1 - 2 * core
    factor = 1.0 / math.sqrt(HEAD)
    depth = t_ref.shape[1]
    width = do_ref.shape[1]
    step = 2 * HEAD // CHUNKS
    hk = CHUNKS // 2
    slab = 2 * HEAD
    cols = [c, flip(c, 1), flip(c, 2), flip(c, 3)]
    to_cols = [(s, r, p) for p in cols]
    to_row = (s, 1 - r, c)
    to_diag = (s, 1 - r, cols[2])

    def wrap(a, n):
        return lax.rem(a + 2 * n, n)

    def dev_z(zz):
        return (y * nz + zz, r, c)

    def dev_y(yy):
        return (yy * nz + z, r, c)

    own_tokens = pltpu.make_async_copy(t_ref, tbuf.at[0], lsem.at[0])
    own_w = pltpu.make_async_copy(w_ref, wv, lsem.at[1])
    own_wo = pltpu.make_async_copy(
        wo_ref.at[:, pl.ds(pl.multiple_of(c * width, 128), width)], wo_v.at[0], lsem.at[2]
    )
    own_do = pltpu.make_async_copy(do_ref, do_v, lsem.at[3])
    own_tokens.start()
    own_w.start()
    own_wo.start()
    own_do.start()
    greet(
        [dev_z(wrap(z + d, nz)) for d in range(1, nz)]
        + [dev_y(wrap(y + d, ny)) for d in range(1, ny)]
        + [(wrap(y + d, ny) * nz + z, 1 - r, c) for d in range(1, ny)]
        + [to_row]
        + to_cols[1:]
        + [to_diag, (s, 1 - r, cols[3])]
    )

    piece = depth // (ny * nz)
    orow = HEAD // nz
    half_width = width // 2

    def w_piece(yy, zz):
        start = pl.multiple_of((yy * nz + zz) * piece, 16)
        return w_x.at[pl.ds(1, 2), pl.ds(start, piece), :]

    def o_piece(zz):
        rows = pl.ds(pl.multiple_of(zz * orow, 16), orow)
        return wo_v.at[pl.ds(2, 2), rows, pl.ds(0, half_width)]

    w_seeds, o_seeds, o_direct = [], [], []
    for h in range(2):
        p = cols[2 + h]
        start = pl.multiple_of(s * piece, 16)
        w_seeds.append(
            remote(
                w_ref.at[pl.ds(pl.multiple_of(p * depth + s * piece, 16), piece), :],
                w_x.at[1 + h, pl.ds(start, piece), :],
                sds.at[0, h],
                sdr.at[0, h],
                to_cols[2 + h],
            )
        )
        orows = pl.ds(pl.multiple_of(z * orow, 16), orow)
        o_seeds.append(
            remote(
                wo_ref.at[orows, pl.ds(pl.multiple_of(p * width, 128), half_width)],
                wo_v.at[2 + h, orows, pl.ds(0, half_width)],
                sds.at[1, h],
                sdr.at[1, h],
                (s, 1 - r, p),
            )
        )
        o_direct.append(
            remote(
                wo_ref.at[:, pl.ds(pl.multiple_of(p * width + half_width, 128), half_width)],
                wo_v.at[2 + h, :, pl.ds(half_width, half_width)],
                sds.at[2, h],
                sdr.at[2, h],
                (s, 1 - r, p),
            )
        )
    seeds = w_seeds + o_seeds + o_direct
    for copy in w_seeds + o_seeds:
        copy.start()

    def rows_of(k):
        start = (1 - r) * HEAD + k * step if k < hk else r * HEAD + (k - hk) * step
        return pl.ds(pl.multiple_of(start, step), step)

    def token_copy(kind, k):
        rows = rows_of(k)
        if kind == 0:
            return remote(
                t_ref.at[rows], tbuf.at[2, rows], tks.at[0, k], tkr.at[0, k], to_cols[2]
            )
        if kind == 1:
            return remote(
                t_ref.at[rows], tbuf.at[1, rows], tks.at[1, k], tkr.at[1, k], to_cols[1]
            )
        return remote(
            tbuf.at[2, rows], tbuf.at[3, rows], tks.at[2, k], tkr.at[2, k], to_cols[1]
        )

    for k in range(CHUNKS):
        token_copy(0, k).start()
        token_copy(1, k).start()
    for copy in o_direct:
        copy.start()

    sib_w = remote(
        w_ref.at[pl.ds(pl.multiple_of(cols[1] * depth, 16), depth), :],
        w_x.at[0],
        sbs.at[0],
        sbr.at[0],
        to_cols[1],
    )
    sib_wo = remote(
        wo_ref.at[:, pl.ds(pl.multiple_of(cols[1] * width, 128), width)],
        wo_v.at[1],
        sbs.at[1],
        sbr.at[1],
        to_cols[1],
    )
    sib_wo.start()
    sib_w.start()

    zl, zsh = ring(nz)
    yl, ysh = ring(ny)
    z_next, z_prev = wrap(z + sgn, nz), wrap(z - sgn, nz)
    y_next, y_prev = wrap(y + sgn, ny), wrap(y - sgn, ny)

    def zq(long, t):
        return wrap(z - sgn * t, nz) if long else wrap(z + sgn * t, nz)

    def yq(long, t):
        return wrap(y - sgn * t, ny) if long else wrap(y + sgn * t, ny)

    def z_ring(pick, snd, rcv, long, t):
        ref = pick(zq(long, t))
        way = 0 if long else 1
        return remote(
            ref, ref, snd.at[way, t], rcv.at[way, t + 1], dev_z(z_next if long else z_prev)
        )

    def z_ring_in(pick, snd, rcv, long, t):
        ref = pick(zq(long, t))
        way = 0 if long else 1
        return remote(ref, ref, snd.at[way, t], rcv.at[way, t], dev_z(z_next))

    def y_ring(pick, snd, rcv, long, t):
        ref = pick(yq(long, t))
        way = 0 if long else 1
        return remote(
            ref, ref, snd.at[way, t], rcv.at[way, t + 1], dev_y(y_next if long else y_prev)
        )

    def y_ring_in(pick, snd, rcv, long, t):
        ref = pick(yq(long, t))
        way = 0 if long else 1
        return remote(ref, ref, snd.at[way, t], rcv.at[way, t], dev_y(y_next))

    started = []

    def go(copy):
        copy.start()
        started.append(copy)

    def w_here(zz):
        return w_piece(y, zz)

    def z_start(pick, snd, rcv):
        if zl:
            go(z_ring(pick, snd, rcv, True, 0))
        if zsh:
            go(z_ring(pick, snd, rcv, False, 0))

    def y_start(pick, snd, rcv):
        if yl:
            go(y_ring(pick, snd, rcv, True, 0))
        if ysh:
            go(y_ring(pick, snd, rcv, False, 0))

    def z_round(pick, snd, rcv, t):
        ways = []
        for long, hops in ((True, zl), (False, zsh)):
            if t <= hops:
                z_ring_in(pick, snd, rcv, long, t).wait_recv()
                if t < hops:
                    go(z_ring(pick, snd, rcv, long, t))
                ways.append(long)
        return ways

    def y_round(pick, snd, rcv, t):
        for long, hops in ((True, yl), (False, ysh)):
            if t <= hops:
                y_ring_in(pick, snd, rcv, long, t).wait_recv()
                if t < hops:
                    go(y_ring(pick, snd, rcv, long, t))

    def w_column(long, t):
        zz = zq(long, t)
        index = t if long else zl + t

        def pick(yy):
            return w_piece(yy, zz)

        return pick, wys.at[index], wyr.at[index]

    def product(i, rows, start):
        return jnp.dot(
            tbuf[i, rows, :],
            wv[pl.ds(pl.multiple_of(start, 16), depth), :],
            preferred_element_type=F32,
        )

    def part_copy(k):
        rows = pl.ds(k * step, step)
        return remote(psend.at[rows], precv.at[rows], pts.at[k], ptr.at[k], to_row)

    def z_rows(zz):
        return pl.ds(pl.multiple_of(zz * HEAD, HEAD), HEAD)

    def q_rows(zz, k):
        return pl.ds(pl.multiple_of(zz * HEAD + k * step, step), step)

    def kv_rows(yy, rr, k):
        return pl.ds(pl.multiple_of(yy * slab + rr * HEAD + k * step, step), step)

    def token_arrival(kind, k):
        ref = tbuf.at[(2, 1, 3)[kind], rows_of(k)]
        remote(ref, ref, tks.at[kind, k], tkr.at[kind, k], to_cols[1]).wait_recv()

    def project_relay(k):
        token_arrival(0, k)
        go(token_copy(2, k))

    def project(k):
        rows = rows_of(k)
        token_arrival(1, k)
        acc = product(0, rows, c * depth) + product(1, rows, cols[1] * depth)
        acc = acc + product(2, rows, cols[2] * depth)
        token_arrival(2, k)
        acc = acc + product(3, rows, cols[3] * depth)
        if k < hk:
            psend[pl.ds(k * step, step), :] = acc
            go(part_copy(k))
        else:
            part_copy(k - hk).wait_recv()
            out = pl.ds((k - hk) * step, step)
            packed = (acc + precv[out, :]).astype(BF)
            q_all[q_rows(z, k - hk), :] = packed[:, :HEAD]
            kv_all[kv_rows(y, r, k - hk), :] = packed[:, HEAD:]

    def kv_row(k):
        rows = kv_rows(y, r, k)
        return remote(kv_all.at[rows], kv_all.at[rows], kvs.at[k, 0], kvr.at[k, 2 * ny], to_row)

    def kv_row_arrival(k):
        rows = kv_rows(y, 1 - r, k)
        return remote(kv_all.at[rows], kv_all.at[rows], kvs.at[k, 0], kvr.at[k, 2 * ny], to_row)

    def kv_send(d, other, k):
        rr = 1 - r if other else r
        rows = kv_rows(y, rr, k)
        return remote(
            kv_all.at[rows],
            kv_all.at[rows],
            kvs.at[k, 1 + 2 * d + other],
            kvr.at[k, 2 * y + other],
            dev_y(wrap(y + d, ny)),
        )

    def kv_arrival(yy, other, k):
        rr = 1 - r if other else r
        rows = kv_rows(yy, rr, k)
        return remote(
            kv_all.at[rows], kv_all.at[rows], kvs.at[k, 0], kvr.at[k, 2 * yy + other], to_row
        )

    def kv_sends(other, k):
        for d in range(1, ny):

            @pl.when(y + d < ny)
            def _():
                kv_send(d, other, k).start()

    def q_send(d, k):
        rows = q_rows(z, k)
        to = wrap(z + d, nz)
        return remote(q_all.at[rows], q_all.at[rows], qs.at[k, d], qr.at[k, d], dev_z(to))

    def q_arrival(d, k):
        rows = q_rows(wrap(z - d, nz), k)
        return remote(q_all.at[rows], q_all.at[rows], qs.at[k, d], qr.at[k, d], dev_z(z_next))

    order = sorted(range(1, nz), key=lambda d: -min(d, nz - d))

    def share(k):
        go(kv_row(k))
        kv_sends(0, k)
        for d in order:
            go(q_send(d, k))

    for copy in w_seeds:
        copy.wait_recv()
    z_start(w_here, wzs, wzr)
    pick, snd, rcv = w_column(True, 0)
    y_start(pick, snd, rcv)
    for copy in o_seeds:
        copy.wait_recv()
    z_start(o_piece, ozs, ozr)
    columns = [[(True, 0)]]
    own_tokens.wait()
    own_w.wait()
    for k in range(max(CHUNKS, zl)):
        t = k + 1
        if k < CHUNKS:
            project_relay(k)
        if t <= zl:
            ways = z_round(w_here, wzs, wzr, t)
            for long in ways:
                y_start(*w_column(long, t))
            columns.append([(long, t) for long in ways])
            for column in columns[t - 1]:
                y_round(*w_column(*column), 1)
            z_round(o_piece, ozs, ozr, t)
        if k < CHUNKS:
            project(k)
        if hk <= k < CHUNKS:
            share(k - hk)

    for column in columns[zl]:
        y_round(*w_column(*column), 1)

    for k in range(hk):
        kv_row_arrival(k).wait_recv()
        kv_sends(1, k)

    own_do.wait()
    own_wo.wait()
    sib_wo.wait_recv()
    for copy in o_direct:
        copy.wait_recv()
    for i in range(1, 4):
        ups[i] = dot_nt(do_v[...], wo_v[i])
        go(remote(ups.at[i], upr.at[i], cs.at[0, i], cr.at[0, i], to_cols[i]))
    upr[0] = dot_nt(do_v[...], wo_v[0])

    for d in order:
        for k in range(hk):
            q_arrival(d, k).wait_recv()
    hz = nz // 2
    hq = hz * HEAD
    near = z // hz
    far = 1 - near
    lane = lax.broadcasted_iota(jnp.int32, (1, hq), 1)
    kofs = lax.broadcasted_iota(jnp.int32, (slab, 1), 0)

    def y_rows(yy):
        return pl.ds(pl.multiple_of(yy * slab, slab), slab)

    def q_half(half):
        return pl.ds(pl.multiple_of(half * hq, hq), hq)

    def z_give(kind, src, dst, to):
        return remote(src.at[to], dst.at[z], zs.at[kind, to], zr.at[kind, z], dev_z(to))

    def z_give_arrival(kind, dst, d):
        slot = wrap(z - d, nz)
        remote(
            dst.at[slot], dst.at[slot], zs.at[kind, slot], zr.at[kind, slot], dev_z(z_next)
        ).wait_recv()

    def u_piece(zz):
        return u_all.at[z_rows(zz)]

    def forward(half, first):
        lanes_of = q_half(half)
        queries = q_all[lanes_of, :]
        qpos = (y * nz + half * hz + lane // HEAD) * slab + r * HEAD + lane % HEAD

        def score_turn(yy, largest):
            if first:

                @pl.when(yy < y)
                def _():
                    for k in range(hk):
                        kv_arrival(yy, 0, k).wait_recv()
                        kv_arrival(yy, 1, k).wait_recv()

            keys = kv_all[y_rows(yy), :HEAD]
            scores = dot_nt(keys, queries) * factor
            kpos = (yy * nz + z) * slab + kofs
            scores = jnp.where(kpos <= qpos, scores, masked_score)
            s_all[y_rows(yy), lanes_of] = scores
            return jnp.maximum(largest, jnp.max(scores, axis=0, keepdims=True))

        largest = lax.fori_loop(0, y + 1, score_turn, jnp.full((1, hq), masked_score, F32))

        def weight_turn(yy, carry):
            total, mixed = carry
            weights = jnp.exp(s_all[y_rows(yy), lanes_of] - largest)
            total = total + jnp.sum(weights, axis=0, keepdims=True)
            mixed = mixed + dot_tn(kv_all[y_rows(yy), HEAD:], weights.astype(BF))
            return total, mixed

        total, mixed = lax.fori_loop(
            0, y + 1, weight_turn, (jnp.zeros((1, hq), F32), jnp.zeros((HEAD, hq), F32))
        )
        for j in range(hz):
            zz = half * hz + j
            lanes = slice(j * HEAD, (j + 1) * HEAD)
            o_snd[zz] = mixed[:, lanes].astype(BF)
            st_snd[zz, 0:1, :] = largest[:, lanes]
            st_snd[zz, 1:2, :] = total[:, lanes]

            @pl.when(zz != z)
            def _():
                z_give(1, o_snd, o_rcv, zz).start()
                z_give(2, st_snd, st_rcv, zz).start()

    forward(far, True)
    for i in range(1, 4):
        remote(upr.at[i], upr.at[i], cs.at[0, i], cr.at[0, i], to_cols[i]).wait_recv()
    up = (upr[0] + upr[1] + upr[2] + upr[3]).astype(BF)
    u_all[z_rows(z), :] = up
    z_start(u_piece, uzs, uzr)
    up_t = up.astype(F32).T
    forward(near, False)
    z_round(u_piece, uzs, uzr, 1)
    o_rcv[z] = o_snd[z]
    st_rcv[z] = st_snd[z]
    z_round(u_piece, uzs, uzr, 2)

    for d in order:
        z_give_arrival(2, st_rcv, d)
    top = st_rcv[0, 0:1, :]
    for zz in range(1, nz):
        top = jnp.maximum(top, st_rcv[zz, 0:1, :])
    full_total = jnp.zeros((1, HEAD), F32)
    for zz in range(nz):
        full_total = full_total + jnp.exp(st_rcv[zz, 0:1, :] - top) * st_rcv[zz, 1:2, :]
    full = jnp.exp(st_rcv[z, 0:1, :] - top) * o_rcv[z].astype(F32)
    for d in order:
        z_give_arrival(1, o_rcv, d)
        slot = wrap(z - d, nz)
        full = full + jnp.exp(st_rcv[slot, 0:1, :] - top) * o_rcv[slot].astype(F32)
    att_t = (full / full_total).astype(BF).astype(F32)
    ld_snd[0:1, :] = top + jnp.log(full_total)
    ld_snd[1:2, :] = jnp.sum(up_t * att_t, axis=0, keepdims=True)
    ld_rcv[z] = ld_snd[...]
    for d in order:
        to = wrap(z + d, nz)
        go(remote(ld_snd, ld_rcv.at[z], zs.at[3, to], zr.at[3, z], dev_z(to)))
    for t in range(3, zl + 1):
        z_round(u_piece, uzs, uzr, t)
    att_all[0] = att_t.T.astype(BF)
    for i in range(1, 4):
        go(remote(att_all.at[0], att_all.at[i], cs.at[1, i], cr.at[1, i], to_cols[i]))

    for d in order:
        z_give_arrival(3, ld_rcv, d)

    def half_rows(yy, rr):
        return pl.ds(pl.multiple_of(yy * slab + rr * HEAD, HEAD), HEAD)

    def dkv_send(yy, rr):
        return remote(
            dkv_snd.at[half_rows(yy, rr)],
            dkv_rcv.at[half_rows(y, r)],
            ds.at[yy, rr],
            dr.at[2 * y + r],
            (yy * nz + z, rr, c),
        )

    def backward(half, first):
        lanes_of = q_half(half)
        queries, upstream = q_all[lanes_of, :], u_all[lanes_of, :]
        logsum = jnp.concatenate([ld_rcv[half * hz + j, 0:1, :] for j in range(hz)], axis=1)
        delta = jnp.concatenate([ld_rcv[half * hz + j, 1:2, :] for j in range(hz)], axis=1)

        def grad_turn(yy, dq):
            keys, values = kv_all[y_rows(yy), :HEAD], kv_all[y_rows(yy), HEAD:]
            probs = jnp.exp(s_all[y_rows(yy), lanes_of] - logsum)
            prob_grad = dot_nt(values, upstream)
            score_grad = (probs * (prob_grad - delta)).astype(BF)
            dk = jnp.dot(score_grad, queries, preferred_element_type=F32) * factor
            dv = jnp.dot(probs.astype(BF), upstream, preferred_element_type=F32)
            if first:
                dkv_own[y_rows(yy), :HEAD] = dk
                dkv_own[y_rows(yy), HEAD:] = dv
            else:
                dk = dk + dkv_own[y_rows(yy), :HEAD]
                dv = dv + dkv_own[y_rows(yy), HEAD:]
                dkv_snd[y_rows(yy), :HEAD] = dk.astype(BF)
                dkv_snd[y_rows(yy), HEAD:] = dv.astype(BF)

                @pl.when(yy < y)
                def _():
                    dkv_send(yy, r).start()

                dkv_send(yy, 1 - r).start()

                @pl.when(yy == y)
                def _():
                    dkv_own[y_rows(yy), :HEAD] = dk
                    dkv_own[y_rows(yy), HEAD:] = dv

            return dq + dot_tn(keys, score_grad)

        dq = lax.fori_loop(0, y + 1, grad_turn, jnp.zeros((HEAD, hq), F32))
        for j in range(hz):
            zz = half * hz + j
            dq_snd[zz] = (dq[:, j * HEAD : (j + 1) * HEAD] * factor).astype(BF)

            @pl.when(zz != z)
            def _():
                z_give(4, dq_snd, dq_rcv, zz).start()

    backward(far, True)
    backward(near, False)

    for i in range(1, 4):
        remote(att_all.at[i], att_all.at[i], cs.at[1, i], cr.at[1, i], to_cols[i]).wait_recv()
    for j in range(4):
        part = width // 4
        lanes = pl.ds(j * part, part)
        total_out = jnp.dot(att_all[0], wo_v[0, :, lanes], preferred_element_type=F32)
        for i in range(1, 4):
            total_out = total_out + jnp.dot(
                att_all[i], wo_v[i, :, lanes], preferred_element_type=F32
            )
        out_ref[:, lanes] = total_out.astype(BF)

    def dp_rows(rr):
        return pl.ds(pl.multiple_of(rr * HEAD, HEAD), HEAD)

    mine = dp_rows(r)
    dq_sum = dq_snd[z].astype(F32)
    for d in order:
        z_give_arrival(4, dq_rcv, d)
        dq_sum = dq_sum + dq_rcv[wrap(z - d, nz)].astype(F32)
    dp_all[0, mine, :HEAD] = dq_sum.T.astype(BF)

    def dkv_arrival(yy, rr):
        ref = dkv_rcv.at[half_rows(yy, rr)]
        remote(ref, ref, ds.at[0, 0], dr.at[2 * yy + rr], to_row).wait_recv()
        dkv_own[half_rows(y, r), :] += dkv_rcv[half_rows(yy, rr), :].astype(F32)

    dkv_arrival(y, 1 - r)
    for d in range(1, ny):

        @pl.when(y + d < ny)
        def _():
            dkv_arrival(wrap(y + d, ny), r)
            dkv_arrival(wrap(y + d, ny), 1 - r)

    dp_all[0, mine, HEAD:] = dkv_own[half_rows(y, r), :].astype(BF)

    peers = [to_cols[2], to_row, to_diag]
    slots = [(2, r), (0, 1 - r), (2, 1 - r)]

    def dp_copy(i):
        dst = dp_all.at[(2, 0, 2, 1)[i], mine]
        return remote(
            dp_all.at[0, mine], dst, gs.at[i], gr.at[i], to_cols[1] if i == 3 else peers[i]
        )

    def dp_relay(i):
        col, rr = slots[i]
        return remote(
            dp_all.at[col, dp_rows(rr)],
            dp_all.at[col + 1, dp_rows(rr)],
            gs.at[4 + i],
            gr.at[4 + i],
            to_cols[1],
        )

    def dp_arrival(i):
        col, rr = (1, r) if i == 3 else slots[i % 4]
        col = col + 1 if i > 3 else col
        ref = dp_all.at[col, dp_rows(rr)]
        remote(ref, ref, gs.at[i], gr.at[i], to_cols[1]).wait_recv()

    for i in (2, 1, 0, 3):
        go(dp_copy(i))

    for t in range(2, yl + 1):
        for round_columns in columns:
            for column in round_columns:
                y_round(*w_column(*column), t)
    sib_w.wait_recv()

    def dx_half(rr):
        rows = dp_rows(rr)
        blk = min(256, depth)

        def turn(j, carry):
            start = pl.multiple_of(j * blk, blk)
            acc = dot_nt(dp_all[0, rows, :], wv[pl.ds(c * depth + start, blk), :])
            for i in range(1, 4):
                acc = acc + dot_nt(dp_all[i, rows, :], w_x[i - 1, pl.ds(start, blk), :])
            dx_ref[rows, pl.ds(start, blk)] = acc.astype(BF)
            return carry

        lax.fori_loop(0, depth // blk, turn, 0)

    dp_arrival(0)
    go(dp_relay(0))
    dp_arrival(1)
    go(dp_relay(1))
    dp_arrival(2)
    go(dp_relay(2))
    dp_arrival(3)
    dp_arrival(4)
    dx_half(r)
    dp_arrival(5)
    dp_arrival(6)
    dx_half(1 - r)

    for d in range(1, ny):

        @pl.when(y + d < ny)
        def _():
            for k in range(hk):
                kv_send(d, 0, k).wait_send()
                kv_send(d, 1, k).wait_send()

    def sent_turn(yy, carry):
        dkv_send(yy, 1 - r).wait_send()

        @pl.when(yy < y)
        def _():
            dkv_send(yy, r).wait_send()

        return carry

    lax.fori_loop(0, y + 1, sent_turn, 0)
    for d in order:
        to = wrap(z + d, nz)
        z_give(1, o_snd, o_rcv, to).wait_send()
        z_give(2, st_snd, st_rcv, to).wait_send()
        z_give(4, dq_snd, dq_rcv, to).wait_send()
    for copy in seeds + [sib_w, sib_wo] + started:
        copy.wait_send()
    for k in range(CHUNKS):
        token_copy(0, k).wait_send()
        token_copy(1, k).wait_send()


def body(nz, tokens, input_weight, output_weight, output_cotangent):
    ny = lax.axis_size("seq") // nz
    rows, depth = tokens.shape
    n = input_weight.shape[1]
    width = output_cotangent.shape[1]
    hbm = pl.BlockSpec(memory_space=pl.ANY)
    vm = pl.BlockSpec(memory_space=pltpu.VMEM)
    nk, nq = ny * 2 * HEAD, nz * HEAD
    V = pltpu.VMEM
    sem = pltpu.SemaphoreType.DMA
    zl, zsh = ring(nz)
    yl, ysh = ring(ny)
    return pl.pallas_call(
        functools.partial(layer_kernel, ny, nz),
        out_shape=(
            jax.ShapeDtypeStruct(output_cotangent.shape, BF),
            jax.ShapeDtypeStruct(tokens.shape, BF),
        ),
        in_specs=[hbm] * 4,
        out_specs=(vm, vm),
        scratch_shapes=[
            V((4, rows, depth), BF),
            V((4 * depth, n), BF),
            V((HEAD, n), F32),
            V((HEAD, n), F32),
            V((3, depth, n), BF),
            V((4, HEAD, width), BF),
            V((nq, HEAD), BF),
            V((nk, 2 * HEAD), BF),
            V((nq, HEAD), BF),
            V((HEAD, width), BF),
            V((4, HEAD, HEAD), F32),
            V((4, HEAD, HEAD), F32),
            V((nk, nq), F32),
            V((nz, HEAD, HEAD), BF),
            V((nz, HEAD, HEAD), BF),
            V((nz, 8, HEAD), F32),
            V((nz, 8, HEAD), F32),
            V((8, HEAD), F32),
            V((nz, 8, HEAD), F32),
            V((4, HEAD, HEAD), BF),
            V((nz, HEAD, HEAD), BF),
            V((nz, HEAD, HEAD), BF),
            V((nk, 2 * HEAD), F32),
            V((nk, 2 * HEAD), BF),
            V((nk, 2 * HEAD), BF),
            V((4, 2 * HEAD, n), BF),
            sem((4,)),
            sem((3, 2)),
            sem((3, 2)),
            sem((2, zl + 1)),
            sem((2, zl + 1)),
            sem((nz, 2, yl + 1)),
            sem((nz, 2, yl + 1)),
            sem((2, zl + 1)),
            sem((2, zl + 1)),
            sem((2,)),
            sem((2,)),
            sem((3, CHUNKS)),
            sem((3, CHUNKS)),
            sem((CHUNKS // 2,)),
            sem((CHUNKS // 2,)),
            sem((CHUNKS // 2, nz)),
            sem((CHUNKS // 2, nz)),
            sem((2, zl + 1)),
            sem((2, zl + 1)),
            sem((5, nz)),
            sem((5, nz)),
            sem((CHUNKS // 2, 2 * ny + 1)),
            sem((CHUNKS // 2, 2 * ny + 1)),
            sem((2, 4)),
            sem((2, 4)),
            sem((ny, 2)),
            sem((2 * ny,)),
            sem((7,)),
            sem((7,)),
        ],
        compiler_params=pltpu.CompilerParams(
            collective_id=0, has_side_effects=True, vmem_limit_bytes=52 * 2**20
        ),
        cost_estimate=pl.CostEstimate(
            flops=6_000_000_000, bytes_accessed=20_000_000, transcendentals=2_000_000
        ),
        name="layer",
    )(tokens, input_weight, output_weight, output_cotangent)


def solution(mesh):
    seq = mesh.shape["seq"]
    nz = 8 if seq % 32 == 0 else seq // 2
    return jax.shard_map(
        functools.partial(body, nz),
        mesh=mesh,
        in_specs=(
            P("seq", ("row", "col")),
            P("row", "col"),
            P("col", None),
            P(("seq", "row"), "col"),
        ),
        out_specs=(P(("seq", "row"), "col"), P("seq", ("row", "col"))),
        check_vma=False,
    )
```

```python
import functools
import math

import jax
import jax.numpy as jnp
from jax import lax
from jax.experimental import pallas as pl
from jax.experimental.pallas import tpu as pltpu
from jax.sharding import PartitionSpec as P

HEAD = 128
MESH = pl.DeviceIdType.MESH
masked_score = -1e30
BF = jnp.bfloat16
F32 = jnp.float32
CHUNKS = 4
AHEAD = 2


def remote(src, dst, send_sem, recv_sem, device):
    return pltpu.make_async_remote_copy(
        src_ref=src,
        dst_ref=dst,
        send_sem=send_sem,
        recv_sem=recv_sem,
        device_id=device,
        device_id_type=MESH,
    )


def greet(devices):
    barrier = pltpu.get_barrier_semaphore()
    for device in devices:
        pl.semaphore_signal(barrier, inc=1, device_id=device, device_id_type=MESH)
    pl.semaphore_wait(barrier, len(devices))


def dot_nt(a, b):
    return lax.dot_general(a, b, (((1,), (1,)), ((), ())), preferred_element_type=F32)


def dot_tn(a, b):
    return lax.dot_general(a, b, (((0,), (0,)), ((), ())), preferred_element_type=F32)


def flip(c, bits):
    low, high = lax.rem(c, 2), c // 2
    if bits & 1:
        low = 1 - low
    if bits & 2:
        high = 1 - high
    return high * 2 + low


def ring(size):
    return size // 2, (size - 1) // 2


def layer_kernel(
    ny,
    nz,
    t_ref,
    w_ref,
    wo_ref,
    do_ref,
    out_ref,
    dx_ref,
    tbuf,
    wv,
    psend,
    precv,
    w_x,
    wo_v,
    q_all,
    kv_all,
    u_all,
    do_v,
    ups,
    upr,
    s_all,
    o_snd,
    o_rcv,
    st_snd,
    st_rcv,
    st_rows,
    o_all,
    o_scale,
    ld,
    att_all,
    dq_snd,
    dq_rcv,
    dkv_own,
    dkv_snd,
    dkv_rcv,
    dp_all,
    dx_acc,
    lsem,
    sds,
    sdr,
    wzs,
    wzr,
    wys,
    wyr,
    ozs,
    ozr,
    sbs,
    sbr,
    tks,
    tkr,
    pts,
    ptr,
    qs,
    qr,
    zs,
    zr,
    kvs,
    kvr,
    cs,
    cr,
    ds,
    dr,
    gs,
    gr,
):
    s, r, c = lax.axis_index("seq"), lax.axis_index("row"), lax.axis_index("col")
    y, z = s // nz, lax.rem(s, nz)
    core = lax.rem(c, 2)
    sgn = 1 - 2 * core
    factor = 1.0 / math.sqrt(HEAD)
    depth = t_ref.shape[1]
    width = do_ref.shape[1]
    step = 2 * HEAD // CHUNKS
    hk = CHUNKS // 2
    slab = 2 * HEAD
    cols = [c, flip(c, 1), flip(c, 2), flip(c, 3)]
    to_cols = [(s, r, p) for p in cols]
    to_row = (s, 1 - r, c)
    to_diag = (s, 1 - r, cols[2])

    def wrap(a, n):
        return lax.rem(a + 2 * n, n)

    def dev_z(zz):
        return (y * nz + zz, r, c)

    def dev_y(yy):
        return (yy * nz + z, r, c)

    own_tokens = pltpu.make_async_copy(t_ref, tbuf.at[0], lsem.at[0])
    own_w = pltpu.make_async_copy(w_ref, wv, lsem.at[1])
    own_wo = pltpu.make_async_copy(
        wo_ref.at[:, pl.ds(pl.multiple_of(c * width, 128), width)], wo_v.at[0], lsem.at[2]
    )
    own_do = pltpu.make_async_copy(do_ref, do_v, lsem.at[3])
    own_tokens.start()
    own_w.start()
    own_wo.start()
    own_do.start()
    greet(
        [dev_z(wrap(z + d, nz)) for d in range(1, nz)]
        + [dev_y(wrap(y + d, ny)) for d in range(1, ny)]
        + [(wrap(y + d, ny) * nz + z, 1 - r, c) for d in range(1, ny)]
        + [to_row]
        + to_cols[1:]
        + [to_diag, (s, 1 - r, cols[3])]
    )

    piece = depth // (ny * nz)
    orow = HEAD // nz
    half_width = width // 2

    def w_piece(yy, zz):
        start = pl.multiple_of((yy * nz + zz) * piece, 16)
        return w_x.at[pl.ds(1, 2), pl.ds(start, piece), :]

    def o_piece(zz):
        rows = pl.ds(pl.multiple_of(zz * orow, 16), orow)
        return wo_v.at[pl.ds(2, 2), rows, pl.ds(0, half_width)]

    w_seeds, o_seeds, o_direct = [], [], []
    for h in range(2):
        p = cols[2 + h]
        start = pl.multiple_of(s * piece, 16)
        w_seeds.append(
            remote(
                w_ref.at[pl.ds(pl.multiple_of(p * depth + s * piece, 16), piece), :],
                w_x.at[1 + h, pl.ds(start, piece), :],
                sds.at[0, h],
                sdr.at[0, h],
                to_cols[2 + h],
            )
        )
        orows = pl.ds(pl.multiple_of(z * orow, 16), orow)
        o_seeds.append(
            remote(
                wo_ref.at[orows, pl.ds(pl.multiple_of(p * width, 128), half_width)],
                wo_v.at[2 + h, orows, pl.ds(0, half_width)],
                sds.at[1, h],
                sdr.at[1, h],
                (s, 1 - r, p),
            )
        )
        o_direct.append(
            remote(
                wo_ref.at[:, pl.ds(pl.multiple_of(p * width + half_width, 128), half_width)],
                wo_v.at[2 + h, :, pl.ds(half_width, half_width)],
                sds.at[2, h],
                sdr.at[2, h],
                (s, 1 - r, p),
            )
        )
    seeds = w_seeds + o_seeds + o_direct
    for copy in w_seeds + o_seeds:
        copy.start()

    def rows_of(k):
        start = (1 - r) * HEAD + k * step if k < hk else r * HEAD + (k - hk) * step
        return pl.ds(pl.multiple_of(start, step), step)

    def token_copy(kind, k):
        rows = rows_of(k)
        if kind == 0:
            return remote(
                t_ref.at[rows], tbuf.at[2, rows], tks.at[0, k], tkr.at[0, k], to_cols[2]
            )
        if kind == 1:
            return remote(
                t_ref.at[rows], tbuf.at[1, rows], tks.at[1, k], tkr.at[1, k], to_cols[1]
            )
        return remote(
            tbuf.at[2, rows], tbuf.at[3, rows], tks.at[2, k], tkr.at[2, k], to_cols[1]
        )

    for k in range(AHEAD):
        token_copy(0, k).start()
    for k in range(CHUNKS):
        token_copy(1, k).start()
    for copy in o_direct:
        copy.start()

    sib_w = remote(
        w_ref.at[pl.ds(pl.multiple_of(cols[1] * depth, 16), depth), :],
        w_x.at[0],
        sbs.at[0],
        sbr.at[0],
        to_cols[1],
    )
    sib_wo = remote(
        wo_ref.at[:, pl.ds(pl.multiple_of(cols[1] * width, 128), width)],
        wo_v.at[1],
        sbs.at[1],
        sbr.at[1],
        to_cols[1],
    )
    sib_wo.start()
    sib_w.start()

    zl, zsh = ring(nz)
    yl, ysh = ring(ny)
    z_next, z_prev = wrap(z + sgn, nz), wrap(z - sgn, nz)
    y_next, y_prev = wrap(y + sgn, ny), wrap(y - sgn, ny)

    def zq(long, t):
        return wrap(z - sgn * t, nz) if long else wrap(z + sgn * t, nz)

    def yq(long, t):
        return wrap(y - sgn * t, ny) if long else wrap(y + sgn * t, ny)

    def z_ring(pick, snd, rcv, long, t):
        ref = pick(zq(long, t))
        way = 0 if long else 1
        return remote(
            ref, ref, snd.at[way, t], rcv.at[way, t + 1], dev_z(z_next if long else z_prev)
        )

    def z_ring_in(pick, snd, rcv, long, t):
        ref = pick(zq(long, t))
        way = 0 if long else 1
        return remote(ref, ref, snd.at[way, t], rcv.at[way, t], dev_z(z_next))

    def y_ring(pick, snd, rcv, long, t):
        ref = pick(yq(long, t))
        way = 0 if long else 1
        return remote(
            ref, ref, snd.at[way, t], rcv.at[way, t + 1], dev_y(y_next if long else y_prev)
        )

    def y_ring_in(pick, snd, rcv, long, t):
        ref = pick(yq(long, t))
        way = 0 if long else 1
        return remote(ref, ref, snd.at[way, t], rcv.at[way, t], dev_y(y_next))

    started = []

    def go(copy):
        copy.start()
        started.append(copy)

    def w_here(zz):
        return w_piece(y, zz)

    def z_start(pick, snd, rcv):
        if zl:
            go(z_ring(pick, snd, rcv, True, 0))
        if zsh:
            go(z_ring(pick, snd, rcv, False, 0))

    def y_start(pick, snd, rcv):
        if yl:
            go(y_ring(pick, snd, rcv, True, 0))
        if ysh:
            go(y_ring(pick, snd, rcv, False, 0))

    def z_round(pick, snd, rcv, t):
        ways = []
        for long, hops in ((True, zl), (False, zsh)):
            if t <= hops:
                z_ring_in(pick, snd, rcv, long, t).wait_recv()
                if t < hops:
                    go(z_ring(pick, snd, rcv, long, t))
                ways.append(long)
        return ways

    def y_round(pick, snd, rcv, t):
        for long, hops in ((True, yl), (False, ysh)):
            if t <= hops:
                y_ring_in(pick, snd, rcv, long, t).wait_recv()
                if t < hops:
                    go(y_ring(pick, snd, rcv, long, t))

    def w_column(long, t):
        zz = zq(long, t)
        index = t if long else zl + t

        def pick(yy):
            return w_piece(yy, zz)

        return pick, wys.at[index], wyr.at[index]

    def product(i, rows, start):
        return jnp.dot(
            tbuf[i, rows, :],
            wv[pl.ds(pl.multiple_of(start, 16), depth), :],
            preferred_element_type=F32,
        )

    def part_copy(k):
        rows = pl.ds(k * step, step)
        return remote(psend.at[rows], precv.at[rows], pts.at[k], ptr.at[k], to_row)

    def z_rows(zz):
        return pl.ds(pl.multiple_of(zz * HEAD, HEAD), HEAD)

    def q_rows(zz, k):
        return pl.ds(pl.multiple_of(zz * HEAD + k * step, step), step)

    def kv_rows(yy, rr, k):
        return pl.ds(pl.multiple_of(yy * slab + rr * HEAD + k * step, step), step)

    def token_arrival(kind, k):
        ref = tbuf.at[(2, 1, 3)[kind], rows_of(k)]
        remote(ref, ref, tks.at[kind, k], tkr.at[kind, k], to_cols[1]).wait_recv()

    def project_relay(k):
        token_arrival(0, k)
        go(token_copy(2, k))

    def project(k):
        rows = rows_of(k)
        token_arrival(1, k)
        acc = product(0, rows, c * depth) + product(1, rows, cols[1] * depth)
        acc = acc + product(2, rows, cols[2] * depth)
        token_arrival(2, k)
        acc = acc + product(3, rows, cols[3] * depth)
        if k < hk:
            psend[pl.ds(k * step, step), :] = acc
            go(part_copy(k))
        else:
            part_copy(k - hk).wait_recv()
            out = pl.ds((k - hk) * step, step)
            packed = (acc + precv[out, :]).astype(BF)
            q_all[q_rows(z, k - hk), :] = packed[:, :HEAD]
            kv_all[kv_rows(y, r, k - hk), :] = packed[:, HEAD:]

    def kv_row(k):
        rows = kv_rows(y, r, k)
        return remote(kv_all.at[rows], kv_all.at[rows], kvs.at[k, 0], kvr.at[k, 2 * ny], to_row)

    def kv_row_arrival(k):
        rows = kv_rows(y, 1 - r, k)
        return remote(kv_all.at[rows], kv_all.at[rows], kvs.at[k, 0], kvr.at[k, 2 * ny], to_row)

    def kv_send(d, other, k):
        rr = 1 - r if other else r
        rows = kv_rows(y, rr, k)
        return remote(
            kv_all.at[rows],
            kv_all.at[rows],
            kvs.at[k, 1 + 2 * d + other],
            kvr.at[k, 2 * y + other],
            dev_y(wrap(y + d, ny)),
        )

    def kv_arrival(yy, other, k):
        rr = 1 - r if other else r
        rows = kv_rows(yy, rr, k)
        return remote(
            kv_all.at[rows], kv_all.at[rows], kvs.at[k, 0], kvr.at[k, 2 * yy + other], to_row
        )

    def kv_sends(other, k):
        for d in range(1, ny):

            @pl.when(y + d < ny)
            def _():
                kv_send(d, other, k).start()

    def q_send(d, k):
        rows = q_rows(z, k)
        to = wrap(z + d, nz)
        return remote(q_all.at[rows], q_all.at[rows], qs.at[k, d], qr.at[k, d], dev_z(to))

    def q_arrival(d, k):
        rows = q_rows(wrap(z - d, nz), k)
        return remote(q_all.at[rows], q_all.at[rows], qs.at[k, d], qr.at[k, d], dev_z(z_next))

    order = sorted(range(1, nz), key=lambda d: -min(d, nz - d))

    def share(k):
        go(kv_row(k))
        kv_sends(0, k)
        for d in order:
            go(q_send(d, k))

    for copy in w_seeds:
        copy.wait_recv()
    z_start(w_here, wzs, wzr)
    pick, snd, rcv = w_column(True, 0)
    y_start(pick, snd, rcv)
    for copy in o_seeds:
        copy.wait_recv()
    z_start(o_piece, ozs, ozr)
    columns = [[(True, 0)]]
    own_tokens.wait()
    own_w.wait()
    for k in range(max(CHUNKS, zl)):
        t = k + 1
        if t <= zl:
            ways = z_round(w_here, wzs, wzr, t)
            for long in ways:
                y_start(*w_column(long, t))
            columns.append([(long, t) for long in ways])
            for column in columns[t - 1]:
                y_round(*w_column(*column), 1)
            z_round(o_piece, ozs, ozr, t)
        if k < CHUNKS:
            project_relay(k)
            if k + AHEAD < CHUNKS:
                token_copy(0, k + AHEAD).start()
            project(k)
        if hk <= k < CHUNKS:
            share(k - hk)

    for column in columns[zl]:
        y_round(*w_column(*column), 1)

    for k in range(hk):
        kv_row_arrival(k).wait_recv()
        kv_sends(1, k)

    own_do.wait()
    own_wo.wait()
    sib_wo.wait_recv()
    for copy in o_direct:
        copy.wait_recv()
    for i in range(1, 4):
        ups[i] = dot_nt(do_v[...], wo_v[i])
        go(remote(ups.at[i], upr.at[i], cs.at[0, i], cr.at[0, i], to_cols[i]))
    upr[0] = dot_nt(do_v[...], wo_v[0])

    for d in order:
        for k in range(hk):
            q_arrival(d, k).wait_recv()
    hz = nz // 2
    hq = hz * HEAD
    near = z // hz
    far = 1 - near
    lane = lax.broadcasted_iota(jnp.int32, (1, hq), 1)
    kofs = lax.broadcasted_iota(jnp.int32, (slab, 1), 0)

    def y_rows(yy):
        return pl.ds(pl.multiple_of(yy * slab, slab), slab)

    def q_half(half):
        return pl.ds(pl.multiple_of(half * hq, hq), hq)

    def z_give(kind, src, dst, to):
        return remote(src.at[to], dst.at[z], zs.at[kind, to], zr.at[kind, z], dev_z(to))

    def z_give_arrival(kind, dst, d):
        slot = wrap(z - d, nz)
        remote(
            dst.at[slot], dst.at[slot], zs.at[kind, slot], zr.at[kind, slot], dev_z(z_next)
        ).wait_recv()

    def score(half, first):
        lanes_of = q_half(half)
        queries = q_all[lanes_of, :]
        qpos = (y * nz + half * hz + lane // HEAD) * slab + r * HEAD + lane % HEAD

        def score_turn(yy, largest):
            if first:

                @pl.when(yy < y)
                def _():
                    for k in range(hk):
                        kv_arrival(yy, 0, k).wait_recv()
                        kv_arrival(yy, 1, k).wait_recv()

            keys = kv_all[y_rows(yy), :HEAD]
            scores = dot_nt(keys, queries) * factor
            kpos = (yy * nz + z) * slab + kofs
            scores = jnp.where(kpos <= qpos, scores, masked_score)
            s_all[y_rows(yy), lanes_of] = scores
            return jnp.maximum(largest, jnp.max(scores, axis=0, keepdims=True))

        return lax.fori_loop(0, y + 1, score_turn, jnp.full((1, hq), masked_score, F32))

    def weigh(half, largest):
        lanes_of = q_half(half)

        def weight_turn(yy, carry):
            total, mixed = carry
            weights = jnp.exp(s_all[y_rows(yy), lanes_of] - largest)
            total = total + jnp.sum(weights, axis=0, keepdims=True)
            mixed = mixed + dot_tn(kv_all[y_rows(yy), HEAD:], weights.astype(BF))
            return total, mixed

        total, mixed = lax.fori_loop(
            0, y + 1, weight_turn, (jnp.zeros((1, hq), F32), jnp.zeros((HEAD, hq), F32))
        )
        st_rows[0:1, lanes_of] = largest
        st_rows[1:2, lanes_of] = total
        o_all[:, lanes_of] = mixed

    top_far = score(far, True)

    for i in range(1, 4):
        remote(upr.at[i], upr.at[i], cs.at[0, i], cr.at[0, i], to_cols[i]).wait_recv()
    u_all[z_rows(z), :] = (upr[0] + upr[1] + upr[2] + upr[3]).astype(BF)
    for d in order:
        to = wrap(z + d, nz)
        rows = z_rows(z)
        go(remote(u_all.at[rows], u_all.at[rows], zs.at[0, to], zr.at[0, z], dev_z(to)))
    top_near = score(near, False)
    weigh(far, top_far)
    weigh(near, top_near)

    for zz in range(nz):
        lanes = slice(zz * HEAD, (zz + 1) * HEAD)
        o_snd[zz] = o_all[:, lanes].astype(BF)
        st_snd[0, zz : zz + 1, :] = st_rows[0:1, lanes]
        st_snd[1, zz : zz + 1, :] = st_rows[1:2, lanes]
    for d in order:
        slot = wrap(z - d, nz)
        ref = u_all.at[z_rows(slot)]
        remote(ref, ref, zs.at[0, slot], zr.at[0, slot], dev_z(z_next)).wait_recv()
    for zz in range(nz):
        lanes = slice(zz * HEAD, (zz + 1) * HEAD)
        up_t = u_all[lanes, :].astype(F32).T
        st_snd[2, zz : zz + 1, :] = jnp.sum(up_t * o_all[:, lanes], axis=0, keepdims=True)

    def st_copy(to):
        return remote(st_snd, st_rcv.at[z], zs.at[2, to], zr.at[2, z], dev_z(to))

    for d in order:
        st_copy(wrap(z + d, nz)).start()
    for d in order:
        z_give(1, o_snd, o_rcv, wrap(z + d, nz)).start()
    o_rcv[z] = o_snd[z]
    st_rcv[z] = st_snd[...]
    for d in order:
        z_give_arrival(2, st_rcv, d)
    top = st_rcv[0, 0]
    for zz in range(1, nz):
        top = jnp.maximum(top, st_rcv[zz, 0])
    full_total = jnp.zeros((nz, HEAD), F32)
    full_delta = jnp.zeros((nz, HEAD), F32)
    for zz in range(nz):
        scale = jnp.exp(st_rcv[zz, 0] - top)
        full_total = full_total + scale * st_rcv[zz, 1]
        full_delta = full_delta + scale * st_rcv[zz, 2]
        o_scale[zz] = scale
    all_logsum = top + jnp.log(full_total)
    all_delta = full_delta / full_total
    for zz in range(nz):
        row = slice(zz, zz + 1)
        ld[zz, 0:1, :] = all_logsum[row]
        ld[zz, 1:2, :] = all_delta[row]
        ld[zz, 2:3, :] = full_total[row]
        for other in range(nz):
            ld[zz, 8 + other : 9 + other, :] = o_scale[other, row, :]

    def half_rows(yy, rr):
        return pl.ds(pl.multiple_of(yy * slab + rr * HEAD, HEAD), HEAD)

    def dkv_send(yy, rr):
        return remote(
            dkv_snd.at[half_rows(yy, rr)],
            dkv_rcv.at[half_rows(y, r)],
            ds.at[yy, rr],
            dr.at[2 * y + r],
            (yy * nz + z, rr, c),
        )

    def backward(half, first):
        lanes_of = q_half(half)
        queries, upstream = q_all[lanes_of, :], u_all[lanes_of, :]
        logsum = jnp.concatenate([ld[half * hz + j, 0:1, :] for j in range(hz)], axis=1)
        delta = jnp.concatenate([ld[half * hz + j, 1:2, :] for j in range(hz)], axis=1)

        def grad_turn(yy, dq):
            keys, values = kv_all[y_rows(yy), :HEAD], kv_all[y_rows(yy), HEAD:]
            probs = jnp.exp(s_all[y_rows(yy), lanes_of] - logsum)
            prob_grad = dot_nt(values, upstream)
            score_grad = (probs * (prob_grad - delta)).astype(BF)
            dk = jnp.dot(score_grad, queries, preferred_element_type=F32) * factor
            dv = jnp.dot(probs.astype(BF), upstream, preferred_element_type=F32)
            if first:
                dkv_own[y_rows(yy), :HEAD] = dk
                dkv_own[y_rows(yy), HEAD:] = dv
            else:
                dk = dk + dkv_own[y_rows(yy), :HEAD]
                dv = dv + dkv_own[y_rows(yy), HEAD:]
                dkv_snd[y_rows(yy), :HEAD] = dk.astype(BF)
                dkv_snd[y_rows(yy), HEAD:] = dv.astype(BF)

                @pl.when(yy < y)
                def _():
                    dkv_send(yy, r).start()

                dkv_send(yy, 1 - r).start()

                @pl.when(yy == y)
                def _():
                    dkv_own[y_rows(yy), :HEAD] = dk
                    dkv_own[y_rows(yy), HEAD:] = dv

            return dq + dot_tn(keys, score_grad)

        dq = lax.fori_loop(0, y + 1, grad_turn, jnp.zeros((HEAD, hq), F32))
        for j in range(hz):
            zz = half * hz + j
            dq_snd[zz] = (dq[:, j * HEAD : (j + 1) * HEAD] * factor).astype(BF)

            @pl.when(zz != z)
            def _():
                z_give(4, dq_snd, dq_rcv, zz).start()

    backward(far, True)
    backward(near, False)

    full = jnp.zeros((HEAD, HEAD), F32)
    for d in order:
        z_give_arrival(1, o_rcv, d)
    for zz in range(nz):
        full = full + ld[z, 8 + zz : 9 + zz, :] * o_rcv[zz].astype(F32)
    att_all[0] = (full / ld[z, 2:3, :]).T.astype(BF)
    for i in range(1, 4):
        go(remote(att_all.at[0], att_all.at[i], cs.at[1, i], cr.at[1, i], to_cols[i]))

    def dp_rows(rr):
        return pl.ds(pl.multiple_of(rr * HEAD, HEAD), HEAD)

    mine, theirs = dp_rows(r), dp_rows(1 - r)

    def dkv_arrival(yy, rr):
        ref = dkv_rcv.at[half_rows(yy, rr)]
        remote(ref, ref, ds.at[0, 0], dr.at[2 * yy + rr], to_row).wait_recv()
        dkv_own[half_rows(y, r), :] += dkv_rcv[half_rows(yy, rr), :].astype(F32)

    for d in range(1, ny):

        @pl.when(y + d < ny)
        def _():
            dkv_arrival(wrap(y + d, ny), r)
            dkv_arrival(wrap(y + d, ny), 1 - r)

    dkv_arrival(y, 1 - r)
    dp_all[0, mine, HEAD:] = dkv_own[half_rows(y, r), :].astype(BF)

    peers = [to_cols[2], to_diag, to_row]
    slots = [(2, r), (2, 1 - r), (0, 1 - r)]
    lanes_of_part = [pl.ds(HEAD, 2 * HEAD), pl.ds(0, HEAD)]

    def dp_ref(col, rr, part):
        return dp_all.at[col, dp_rows(rr), lanes_of_part[part]]

    def dp_copy(i, part):
        return remote(
            dp_ref(0, r, part),
            dp_ref((2, 2, 0, 1)[i], r, part),
            gs.at[part, i],
            gr.at[part, i],
            to_cols[1] if i == 3 else peers[i],
        )

    def dp_relay(i, part):
        col, rr = slots[i]
        return remote(
            dp_ref(col, rr, part),
            dp_ref(col + 1, rr, part),
            gs.at[part, 4 + i],
            gr.at[part, 4 + i],
            to_cols[1],
        )

    def dp_arrival(i, part):
        col, rr = (1, r) if i == 3 else slots[i % 4]
        ref = dp_ref(col + 1 if i > 3 else col, rr, part)
        remote(ref, ref, gs.at[part, i], gr.at[part, i], to_cols[1]).wait_recv()

    for i in range(4):
        go(dp_copy(i, 0))
    dq_sum = dq_snd[z].astype(F32)
    for d in order:
        z_give_arrival(4, dq_rcv, d)
        dq_sum = dq_sum + dq_rcv[wrap(z - d, nz)].astype(F32)
    dp_all[0, mine, :HEAD] = dq_sum.T.astype(BF)
    for i in range(4):
        go(dp_copy(i, 1))

    for t in range(2, yl + 1):
        for round_columns in columns:
            for column in round_columns:
                y_round(*w_column(*column), t)
    sib_w.wait_recv()

    blk = min(512, depth)

    def dx_add(i, rows, first=False, last=False):
        def turn(j, carry):
            start = pl.multiple_of(j * blk, blk)
            out = pl.ds(start, blk)
            weight = wv[pl.ds(c * depth + start, blk), :] if i == 0 else w_x[i - 1, out, :]
            acc = dot_nt(dp_all[i, rows, :], weight)
            if not first:
                acc = acc + dx_acc[rows, out]
            if last:
                dx_ref[rows, out] = acc.astype(BF)
            else:
                dx_acc[rows, out] = acc
            return carry

        lax.fori_loop(0, depth // blk, turn, 0)

    dx_add(0, mine, first=True)
    dp_arrival(3, 0)
    dp_arrival(3, 1)
    dx_add(1, mine)
    for part in range(2):
        for i in range(3):
            dp_arrival(i, part)
            go(dp_relay(i, part))
    for i in range(1, 4):
        remote(att_all.at[i], att_all.at[i], cs.at[1, i], cr.at[1, i], to_cols[i]).wait_recv()
    for j in range(4):
        part = width // 4
        lanes = pl.ds(j * part, part)
        total_out = jnp.dot(att_all[0], wo_v[0, :, lanes], preferred_element_type=F32)
        for i in range(1, 4):
            total_out = total_out + jnp.dot(
                att_all[i], wo_v[i, :, lanes], preferred_element_type=F32
            )
        out_ref[:, lanes] = total_out.astype(BF)
    dx_add(2, mine)
    dx_add(0, theirs, first=True)
    dx_add(2, theirs)
    for i, col, rows, last in ((4, 3, mine, True), (6, 1, theirs, False), (5, 3, theirs, True)):
        dp_arrival(i, 0)
        dp_arrival(i, 1)
        dx_add(col, rows, last=last)

    for d in range(1, ny):

        @pl.when(y + d < ny)
        def _():
            for k in range(hk):
                kv_send(d, 0, k).wait_send()
                kv_send(d, 1, k).wait_send()

    def sent_turn(yy, carry):
        dkv_send(yy, 1 - r).wait_send()

        @pl.when(yy < y)
        def _():
            dkv_send(yy, r).wait_send()

        return carry

    lax.fori_loop(0, y + 1, sent_turn, 0)
    for d in order:
        to = wrap(z + d, nz)
        z_give(1, o_snd, o_rcv, to).wait_send()
        st_copy(to).wait_send()
        z_give(4, dq_snd, dq_rcv, to).wait_send()
    for copy in seeds + [sib_w, sib_wo] + started:
        copy.wait_send()
    for k in range(CHUNKS):
        token_copy(0, k).wait_send()
        token_copy(1, k).wait_send()


def body(nz, tokens, input_weight, output_weight, output_cotangent):
    ny = lax.axis_size("seq") // nz
    rows, depth = tokens.shape
    n = input_weight.shape[1]
    width = output_cotangent.shape[1]
    hbm = pl.BlockSpec(memory_space=pl.ANY)
    vm = pl.BlockSpec(memory_space=pltpu.VMEM)
    nk, nq = ny * 2 * HEAD, nz * HEAD
    V = pltpu.VMEM
    sem = pltpu.SemaphoreType.DMA
    zl, zsh = ring(nz)
    yl, ysh = ring(ny)
    return pl.pallas_call(
        functools.partial(layer_kernel, ny, nz),
        out_shape=(
            jax.ShapeDtypeStruct(output_cotangent.shape, BF),
            jax.ShapeDtypeStruct(tokens.shape, BF),
        ),
        in_specs=[hbm] * 4,
        out_specs=(vm, vm),
        scratch_shapes=[
            V((4, rows, depth), BF),
            V((4 * depth, n), BF),
            V((HEAD, n), F32),
            V((HEAD, n), F32),
            V((3, depth, n), BF),
            V((4, HEAD, width), BF),
            V((nq, HEAD), BF),
            V((nk, 2 * HEAD), BF),
            V((nq, HEAD), BF),
            V((HEAD, width), BF),
            V((4, HEAD, HEAD), F32),
            V((4, HEAD, HEAD), F32),
            V((nk, nq), F32),
            V((nz, HEAD, HEAD), BF),
            V((nz, HEAD, HEAD), BF),
            V((3, nz, HEAD), F32),
            V((nz, 3, nz, HEAD), F32),
            V((8, nq), F32),
            V((HEAD, nq), F32),
            V((nz, nz, HEAD), F32),
            V((nz, 16, HEAD), F32),
            V((4, HEAD, HEAD), BF),
            V((nz, HEAD, HEAD), BF),
            V((nz, HEAD, HEAD), BF),
            V((nk, 2 * HEAD), F32),
            V((nk, 2 * HEAD), BF),
            V((nk, 2 * HEAD), BF),
            V((4, 2 * HEAD, n), BF),
            V(tokens.shape, F32),
            sem((4,)),
            sem((3, 2)),
            sem((3, 2)),
            sem((2, zl + 1)),
            sem((2, zl + 1)),
            sem((nz, 2, yl + 1)),
            sem((nz, 2, yl + 1)),
            sem((2, zl + 1)),
            sem((2, zl + 1)),
            sem((2,)),
            sem((2,)),
            sem((3, CHUNKS)),
            sem((3, CHUNKS)),
            sem((CHUNKS // 2,)),
            sem((CHUNKS // 2,)),
            sem((CHUNKS // 2, nz)),
            sem((CHUNKS // 2, nz)),
            sem((5, nz)),
            sem((5, nz)),
            sem((CHUNKS // 2, 2 * ny + 1)),
            sem((CHUNKS // 2, 2 * ny + 1)),
            sem((2, 4)),
            sem((2, 4)),
            sem((ny, 2)),
            sem((2 * ny,)),
            sem((2, 7)),
            sem((2, 7)),
        ],
        compiler_params=pltpu.CompilerParams(
            collective_id=0, has_side_effects=True, vmem_limit_bytes=52 * 2**20
        ),
        cost_estimate=pl.CostEstimate(
            flops=6_000_000_000, bytes_accessed=20_000_000, transcendentals=2_000_000
        ),
        name="layer",
    )(tokens, input_weight, output_weight, output_cotangent)


def solution(mesh):
    seq = mesh.shape["seq"]
    nz = 8 if seq % 32 == 0 else seq // 2
    return jax.shard_map(
        functools.partial(body, nz),
        mesh=mesh,
        in_specs=(
            P("seq", ("row", "col")),
            P("row", "col"),
            P("col", None),
            P(("seq", "row"), "col"),
        ),
        out_specs=(P(("seq", "row"), "col"), P("seq", ("row", "col"))),
        check_vma=False,
    )
```

```python
import functools
import math

import jax
import jax.numpy as jnp
from jax import lax
from jax.experimental import pallas as pl
from jax.experimental.pallas import tpu as pltpu
from jax.sharding import PartitionSpec as P

HEAD = 128
MESH = pl.DeviceIdType.MESH
masked_score = -1e30
BF = jnp.bfloat16
F32 = jnp.float32
CHUNKS = 4
AHEAD = 2


def remote(src, dst, send_sem, recv_sem, device):
    return pltpu.make_async_remote_copy(
        src_ref=src,
        dst_ref=dst,
        send_sem=send_sem,
        recv_sem=recv_sem,
        device_id=device,
        device_id_type=MESH,
    )


def greet(devices):
    barrier = pltpu.get_barrier_semaphore()
    for device in devices:
        pl.semaphore_signal(barrier, inc=1, device_id=device, device_id_type=MESH)
    pl.semaphore_wait(barrier, len(devices))


def dot_nt(a, b):
    return lax.dot_general(a, b, (((1,), (1,)), ((), ())), preferred_element_type=F32)


def dot_tn(a, b):
    return lax.dot_general(a, b, (((0,), (0,)), ((), ())), preferred_element_type=F32)


def flip(c, bits):
    low, high = lax.rem(c, 2), c // 2
    if bits & 1:
        low = 1 - low
    if bits & 2:
        high = 1 - high
    return high * 2 + low


def ring(size):
    return size // 2, (size - 1) // 2


def layer_kernel(
    ny,
    nz,
    t_ref,
    w_ref,
    wo_ref,
    do_ref,
    out_ref,
    dx_ref,
    tbuf,
    wv,
    psend,
    precv,
    w_x,
    wo_v,
    q_all,
    kv_all,
    u_all,
    do_v,
    ups,
    upr,
    up_own,
    s_all,
    o_snd,
    o_rcv,
    st_snd,
    st_rcv,
    st_rows,
    o_all,
    o_scale,
    ld,
    att_all,
    dq_snd,
    dq_rcv,
    dkv_own,
    dkv_snd,
    dkv_rcv,
    dp_all,
    dx_acc,
    lsem,
    sds,
    sdr,
    wzs,
    wzr,
    wys,
    wyr,
    ozs,
    ozr,
    sbs,
    sbr,
    tks,
    tkr,
    pts,
    ptr,
    qs,
    qr,
    zs,
    zr,
    kvs,
    kvr,
    cs,
    cr,
    ds,
    dr,
    gs,
    gr,
):
    s, r, c = lax.axis_index("seq"), lax.axis_index("row"), lax.axis_index("col")
    y, z = s // nz, lax.rem(s, nz)
    core = lax.rem(c, 2)
    sgn = 1 - 2 * core
    factor = 1.0 / math.sqrt(HEAD)
    depth = t_ref.shape[1]
    width = do_ref.shape[1]
    step = 2 * HEAD // CHUNKS
    hk = CHUNKS // 2
    slab = 2 * HEAD
    cols = [c, flip(c, 1), flip(c, 2), flip(c, 3)]
    to_cols = [(s, r, p) for p in cols]
    to_row = (s, 1 - r, c)
    to_diag = (s, 1 - r, cols[2])

    def wrap(a, n):
        return lax.rem(a + 2 * n, n)

    def dev_z(zz):
        return (y * nz + zz, r, c)

    def dev_y(yy):
        return (yy * nz + z, r, c)

    own_tokens = pltpu.make_async_copy(t_ref, tbuf.at[0], lsem.at[0])
    own_w = pltpu.make_async_copy(w_ref, wv, lsem.at[1])
    own_wo = pltpu.make_async_copy(
        wo_ref.at[:, pl.ds(pl.multiple_of(c * width, 128), width)], wo_v.at[0], lsem.at[2]
    )
    own_do = pltpu.make_async_copy(do_ref, do_v, lsem.at[3])
    own_tokens.start()
    own_w.start()
    own_wo.start()
    own_do.start()
    greet(
        [dev_z(wrap(z + d, nz)) for d in range(1, nz)]
        + [dev_y(wrap(y + d, ny)) for d in range(1, ny)]
        + [(wrap(y + d, ny) * nz + z, 1 - r, c) for d in range(1, ny)]
        + [to_row]
        + to_cols[1:]
        + [to_diag, (s, 1 - r, cols[3])]
    )

    piece = depth // (ny * nz)
    orow = HEAD // nz
    half_width = width // 2

    def w_piece(yy, zz):
        start = pl.multiple_of((yy * nz + zz) * piece, 16)
        return w_x.at[pl.ds(1, 2), pl.ds(start, piece), :]

    def o_piece(zz):
        rows = pl.ds(pl.multiple_of(zz * orow, 16), orow)
        return wo_v.at[pl.ds(2, 2), rows, pl.ds(0, half_width)]

    w_seeds, o_seeds, o_direct = [], [], []
    for h in range(2):
        p = cols[2 + h]
        start = pl.multiple_of(s * piece, 16)
        w_seeds.append(
            remote(
                w_ref.at[pl.ds(pl.multiple_of(p * depth + s * piece, 16), piece), :],
                w_x.at[1 + h, pl.ds(start, piece), :],
                sds.at[0, h],
                sdr.at[0, h],
                to_cols[2 + h],
            )
        )
        orows = pl.ds(pl.multiple_of(z * orow, 16), orow)
        o_seeds.append(
            remote(
                wo_ref.at[orows, pl.ds(pl.multiple_of(p * width, 128), half_width)],
                wo_v.at[2 + h, orows, pl.ds(0, half_width)],
                sds.at[1, h],
                sdr.at[1, h],
                (s, 1 - r, p),
            )
        )
        o_direct.append(
            remote(
                wo_ref.at[:, pl.ds(pl.multiple_of(p * width + half_width, 128), half_width)],
                wo_v.at[2 + h, :, pl.ds(half_width, half_width)],
                sds.at[2, h],
                sdr.at[2, h],
                (s, 1 - r, p),
            )
        )
    seeds = w_seeds + o_seeds + o_direct
    for copy in w_seeds + o_seeds + o_direct:
        copy.start()

    def rows_of(k):
        start = (1 - r) * HEAD + k * step if k < hk else r * HEAD + (k - hk) * step
        return pl.ds(pl.multiple_of(start, step), step)

    def token_copy(kind, k):
        rows = rows_of(k)
        if kind == 0:
            return remote(
                t_ref.at[rows], tbuf.at[2, rows], tks.at[0, k], tkr.at[0, k], to_cols[2]
            )
        if kind == 1:
            return remote(
                t_ref.at[rows], tbuf.at[1, rows], tks.at[1, k], tkr.at[1, k], to_cols[1]
            )
        return remote(
            tbuf.at[2, rows], tbuf.at[3, rows], tks.at[2, k], tkr.at[2, k], to_cols[1]
        )

    for k in range(AHEAD):
        token_copy(0, k).start()
    for k in range(CHUNKS):
        token_copy(1, k).start()
    sib_w = remote(
        w_ref.at[pl.ds(pl.multiple_of(cols[1] * depth, 16), depth), :],
        w_x.at[0],
        sbs.at[0],
        sbr.at[0],
        to_cols[1],
    )
    sib_wo = remote(
        wo_ref.at[:, pl.ds(pl.multiple_of(cols[1] * width, 128), width)],
        wo_v.at[1],
        sbs.at[1],
        sbr.at[1],
        to_cols[1],
    )
    sib_wo.start()
    sib_w.start()

    zl, zsh = ring(nz)
    yl, ysh = ring(ny)
    z_next, z_prev = wrap(z + sgn, nz), wrap(z - sgn, nz)
    y_next, y_prev = wrap(y + sgn, ny), wrap(y - sgn, ny)

    def zq(long, t):
        return wrap(z - sgn * t, nz) if long else wrap(z + sgn * t, nz)

    def yq(long, t):
        return wrap(y - sgn * t, ny) if long else wrap(y + sgn * t, ny)

    def z_ring(pick, snd, rcv, long, t):
        ref = pick(zq(long, t))
        way = 0 if long else 1
        return remote(
            ref, ref, snd.at[way, t], rcv.at[way, t + 1], dev_z(z_next if long else z_prev)
        )

    def z_ring_in(pick, snd, rcv, long, t):
        ref = pick(zq(long, t))
        way = 0 if long else 1
        return remote(ref, ref, snd.at[way, t], rcv.at[way, t], dev_z(z_next))

    def y_ring(pick, snd, rcv, long, t):
        ref = pick(yq(long, t))
        way = 0 if long else 1
        return remote(
            ref, ref, snd.at[way, t], rcv.at[way, t + 1], dev_y(y_next if long else y_prev)
        )

    def y_ring_in(pick, snd, rcv, long, t):
        ref = pick(yq(long, t))
        way = 0 if long else 1
        return remote(ref, ref, snd.at[way, t], rcv.at[way, t], dev_y(y_next))

    started = []

    def go(copy):
        copy.start()
        started.append(copy)

    def w_here(zz):
        return w_piece(y, zz)

    def z_start(pick, snd, rcv):
        if zl:
            go(z_ring(pick, snd, rcv, True, 0))
        if zsh:
            go(z_ring(pick, snd, rcv, False, 0))

    def y_start(pick, snd, rcv):
        if yl:
            go(y_ring(pick, snd, rcv, True, 0))
        if ysh:
            go(y_ring(pick, snd, rcv, False, 0))

    def z_round(pick, snd, rcv, t):
        ways = []
        for long, hops in ((True, zl), (False, zsh)):
            if t <= hops:
                z_ring_in(pick, snd, rcv, long, t).wait_recv()
                if t < hops:
                    go(z_ring(pick, snd, rcv, long, t))
                ways.append(long)
        return ways

    def y_round(pick, snd, rcv, t):
        for long, hops in ((True, yl), (False, ysh)):
            if t <= hops:
                y_ring_in(pick, snd, rcv, long, t).wait_recv()
                if t < hops:
                    go(y_ring(pick, snd, rcv, long, t))

    def w_column(long, t):
        zz = zq(long, t)
        index = t if long else zl + t

        def pick(yy):
            return w_piece(yy, zz)

        return pick, wys.at[index], wyr.at[index]

    def product(i, rows, start):
        return jnp.dot(
            tbuf[i, rows, :],
            wv[pl.ds(pl.multiple_of(start, 16), depth), :],
            preferred_element_type=F32,
        )

    def part_copy(k):
        rows = pl.ds(k * step, step)
        return remote(psend.at[rows], precv.at[rows], pts.at[k], ptr.at[k], to_row)

    def z_rows(zz):
        return pl.ds(pl.multiple_of(zz * HEAD, HEAD), HEAD)

    def q_rows(zz, k):
        return pl.ds(pl.multiple_of(zz * HEAD + k * step, step), step)

    def kv_rows(yy, rr, k):
        return pl.ds(pl.multiple_of(yy * slab + rr * HEAD + k * step, step), step)

    def token_arrival(kind, k):
        ref = tbuf.at[(2, 1, 3)[kind], rows_of(k)]
        remote(ref, ref, tks.at[kind, k], tkr.at[kind, k], to_cols[1]).wait_recv()

    def project_relay(k):
        token_arrival(0, k)
        go(token_copy(2, k))

    def project(k):
        rows = rows_of(k)
        token_arrival(1, k)
        acc = product(0, rows, c * depth) + product(1, rows, cols[1] * depth)
        acc = acc + product(2, rows, cols[2] * depth)
        token_arrival(2, k)
        acc = acc + product(3, rows, cols[3] * depth)
        if k < hk:
            psend[pl.ds(k * step, step), :] = acc
            go(part_copy(k))
        else:
            part_copy(k - hk).wait_recv()
            out = pl.ds((k - hk) * step, step)
            packed = (acc + precv[out, :]).astype(BF)
            q_all[q_rows(z, k - hk), :] = packed[:, :HEAD]
            kv_all[kv_rows(y, r, k - hk), :] = packed[:, HEAD:]

    def kv_row(k):
        rows = kv_rows(y, r, k)
        return remote(kv_all.at[rows], kv_all.at[rows], kvs.at[k, 0], kvr.at[k, 2 * ny], to_row)

    def kv_row_arrival(k):
        rows = kv_rows(y, 1 - r, k)
        return remote(kv_all.at[rows], kv_all.at[rows], kvs.at[k, 0], kvr.at[k, 2 * ny], to_row)

    def kv_send(d, other, k):
        rr = 1 - r if other else r
        rows = kv_rows(y, rr, k)
        return remote(
            kv_all.at[rows],
            kv_all.at[rows],
            kvs.at[k, 1 + 2 * d + other],
            kvr.at[k, 2 * y + other],
            dev_y(wrap(y + d, ny)),
        )

    def kv_arrival(yy, other, k):
        rr = 1 - r if other else r
        rows = kv_rows(yy, rr, k)
        return remote(
            kv_all.at[rows], kv_all.at[rows], kvs.at[k, 0], kvr.at[k, 2 * yy + other], to_row
        )

    def kv_sends(other, k):
        for d in range(1, ny):

            @pl.when(y + d < ny)
            def _():
                kv_send(d, other, k).start()

    def q_send(d, k):
        rows = q_rows(z, k)
        to = wrap(z + d, nz)
        return remote(q_all.at[rows], q_all.at[rows], qs.at[k, d], qr.at[k, d], dev_z(to))

    def q_arrival(d, k):
        rows = q_rows(wrap(z - d, nz), k)
        return remote(q_all.at[rows], q_all.at[rows], qs.at[k, d], qr.at[k, d], dev_z(z_next))

    order = sorted(range(1, nz), key=lambda d: -min(d, nz - d))

    def share(k):
        go(kv_row(k))
        kv_sends(0, k)
        for d in order:
            go(q_send(d, k))

    def upstream_terms():
        own_do.wait()
        own_wo.wait()
        for copy in o_direct:
            copy.wait_recv()
        for i in (2, 3):
            ups[i] = dot_nt(do_v[...], wo_v[i])
            go(remote(ups.at[i], upr.at[i], cs.at[0, i], cr.at[0, i], to_cols[i]))
        sib_wo.wait_recv()
        ups[1] = dot_nt(do_v[...], wo_v[1])
        go(remote(ups.at[1], upr.at[1], cs.at[0, 1], cr.at[0, 1], to_cols[1]))
        up_own[...] = dot_nt(do_v[...], wo_v[0])

    for copy in w_seeds:
        copy.wait_recv()
    z_start(w_here, wzs, wzr)
    pick, snd, rcv = w_column(True, 0)
    y_start(pick, snd, rcv)
    for copy in o_seeds:
        copy.wait_recv()
    z_start(o_piece, ozs, ozr)
    columns = [[(True, 0)]]
    own_tokens.wait()
    own_w.wait()
    for k in range(max(CHUNKS, zl)):
        t = k + 1
        if t <= zl:
            ways = z_round(w_here, wzs, wzr, t)
            for long in ways:
                y_start(*w_column(long, t))
            columns.append([(long, t) for long in ways])
            for column in columns[t - 1]:
                y_round(*w_column(*column), 1)
            z_round(o_piece, ozs, ozr, t)
        if k < CHUNKS:
            project_relay(k)
            if k + AHEAD < CHUNKS:
                token_copy(0, k + AHEAD).start()
            if k == CHUNKS - 1:
                upstream_terms()
            project(k)
        if hk <= k < CHUNKS:
            share(k - hk)

    for k in range(hk):
        kv_row_arrival(k).wait_recv()
        kv_sends(1, k)

    for i in range(1, 4):
        remote(upr.at[i], upr.at[i], cs.at[0, i], cr.at[0, i], to_cols[i]).wait_recv()
    up = up_own[...]
    for i in range(1, 4):
        up = up + upr[i]
    u_all[z_rows(z), :] = up.astype(BF)
    for d in order:
        to = wrap(z + d, nz)
        rows = z_rows(z)
        go(remote(u_all.at[rows], u_all.at[rows], zs.at[0, to], zr.at[0, z], dev_z(to)))
    for column in columns[zl]:
        y_round(*w_column(*column), 1)

    for d in order:
        for k in range(hk):
            q_arrival(d, k).wait_recv()
    hz = nz // 2
    hq = hz * HEAD
    near = z // hz
    far = 1 - near
    lane = lax.broadcasted_iota(jnp.int32, (1, hq), 1)
    kofs = lax.broadcasted_iota(jnp.int32, (slab, 1), 0)

    def y_rows(yy):
        return pl.ds(pl.multiple_of(yy * slab, slab), slab)

    def q_half(half):
        return pl.ds(pl.multiple_of(half * hq, hq), hq)

    def z_give(kind, src, dst, to):
        return remote(src.at[to], dst.at[z], zs.at[kind, to], zr.at[kind, z], dev_z(to))

    def z_give_arrival(kind, dst, d):
        slot = wrap(z - d, nz)
        remote(
            dst.at[slot], dst.at[slot], zs.at[kind, slot], zr.at[kind, slot], dev_z(z_next)
        ).wait_recv()

    def score(half, first):
        lanes_of = q_half(half)
        queries = q_all[lanes_of, :]
        qpos = (y * nz + half * hz + lane // HEAD) * slab + r * HEAD + lane % HEAD

        def score_turn(yy, largest):
            if first:

                @pl.when(yy < y)
                def _():
                    for k in range(hk):
                        kv_arrival(yy, 0, k).wait_recv()
                        kv_arrival(yy, 1, k).wait_recv()

            keys = kv_all[y_rows(yy), :HEAD]
            scores = dot_nt(keys, queries) * factor
            kpos = (yy * nz + z) * slab + kofs
            scores = jnp.where(kpos <= qpos, scores, masked_score)
            s_all[y_rows(yy), lanes_of] = scores
            return jnp.maximum(largest, jnp.max(scores, axis=0, keepdims=True))

        return lax.fori_loop(0, y + 1, score_turn, jnp.full((1, hq), masked_score, F32))

    def weigh(half, largest):
        lanes_of = q_half(half)

        def weight_turn(yy, carry):
            total, mixed = carry
            weights = jnp.exp(s_all[y_rows(yy), lanes_of] - largest)
            total = total + jnp.sum(weights, axis=0, keepdims=True)
            mixed = mixed + dot_tn(kv_all[y_rows(yy), HEAD:], weights.astype(BF))
            return total, mixed

        total, mixed = lax.fori_loop(
            0, y + 1, weight_turn, (jnp.zeros((1, hq), F32), jnp.zeros((HEAD, hq), F32))
        )
        st_rows[0:1, lanes_of] = largest
        st_rows[1:2, lanes_of] = total
        o_all[:, lanes_of] = mixed

    top_far = score(far, True)
    top_near = score(near, False)

    weigh(far, top_far)
    weigh(near, top_near)

    for zz in range(nz):
        lanes = slice(zz * HEAD, (zz + 1) * HEAD)
        o_snd[zz] = o_all[:, lanes].astype(BF)
        st_snd[0, zz : zz + 1, :] = st_rows[0:1, lanes]
        st_snd[1, zz : zz + 1, :] = st_rows[1:2, lanes]
    for d in order:
        slot = wrap(z - d, nz)
        ref = u_all.at[z_rows(slot)]
        remote(ref, ref, zs.at[0, slot], zr.at[0, slot], dev_z(z_next)).wait_recv()
    for zz in range(nz):
        lanes = slice(zz * HEAD, (zz + 1) * HEAD)
        up_t = u_all[lanes, :].astype(F32).T
        st_snd[2, zz : zz + 1, :] = jnp.sum(up_t * o_all[:, lanes], axis=0, keepdims=True)

    def st_copy(to):
        return remote(st_snd, st_rcv.at[z], zs.at[2, to], zr.at[2, z], dev_z(to))

    for d in order:
        st_copy(wrap(z + d, nz)).start()
    for d in order:
        z_give(1, o_snd, o_rcv, wrap(z + d, nz)).start()
    o_rcv[z] = o_snd[z]
    st_rcv[z] = st_snd[...]
    for d in order:
        z_give_arrival(2, st_rcv, d)
    top = st_rcv[0, 0]
    for zz in range(1, nz):
        top = jnp.maximum(top, st_rcv[zz, 0])
    full_total = jnp.zeros((nz, HEAD), F32)
    full_delta = jnp.zeros((nz, HEAD), F32)
    for zz in range(nz):
        scale = jnp.exp(st_rcv[zz, 0] - top)
        full_total = full_total + scale * st_rcv[zz, 1]
        full_delta = full_delta + scale * st_rcv[zz, 2]
        o_scale[zz] = scale
    all_logsum = top + jnp.log(full_total)
    all_delta = full_delta / full_total
    for zz in range(nz):
        row = slice(zz, zz + 1)
        ld[zz, 0:1, :] = all_logsum[row]
        ld[zz, 1:2, :] = all_delta[row]
        ld[zz, 2:3, :] = full_total[row]
        for other in range(nz):
            ld[zz, 8 + other : 9 + other, :] = o_scale[other, row, :]

    def half_rows(yy, rr):
        return pl.ds(pl.multiple_of(yy * slab + rr * HEAD, HEAD), HEAD)

    def dkv_send(yy, rr):
        return remote(
            dkv_snd.at[half_rows(yy, rr)],
            dkv_rcv.at[half_rows(y, r)],
            ds.at[yy, rr],
            dr.at[2 * y + r],
            (yy * nz + z, rr, c),
        )

    def backward(half, first):
        lanes_of = q_half(half)
        queries, upstream = q_all[lanes_of, :], u_all[lanes_of, :]
        logsum = jnp.concatenate([ld[half * hz + j, 0:1, :] for j in range(hz)], axis=1)
        delta = jnp.concatenate([ld[half * hz + j, 1:2, :] for j in range(hz)], axis=1)

        def grad_turn(yy, dq):
            keys, values = kv_all[y_rows(yy), :HEAD], kv_all[y_rows(yy), HEAD:]
            probs = jnp.exp(s_all[y_rows(yy), lanes_of] - logsum)
            prob_grad = dot_nt(values, upstream)
            score_grad = (probs * (prob_grad - delta)).astype(BF)
            dk = jnp.dot(score_grad, queries, preferred_element_type=F32) * factor
            dv = jnp.dot(probs.astype(BF), upstream, preferred_element_type=F32)
            if first:
                dkv_own[y_rows(yy), :HEAD] = dk
                dkv_own[y_rows(yy), HEAD:] = dv
            else:
                dk = dk + dkv_own[y_rows(yy), :HEAD]
                dv = dv + dkv_own[y_rows(yy), HEAD:]
                dkv_snd[y_rows(yy), :HEAD] = dk.astype(BF)
                dkv_snd[y_rows(yy), HEAD:] = dv.astype(BF)

                @pl.when(yy < y)
                def _():
                    dkv_send(yy, r).start()

                dkv_send(yy, 1 - r).start()

                @pl.when(yy == y)
                def _():
                    dkv_own[y_rows(yy), :HEAD] = dk
                    dkv_own[y_rows(yy), HEAD:] = dv

            return dq + dot_tn(keys, score_grad)

        dq = lax.fori_loop(0, y + 1, grad_turn, jnp.zeros((HEAD, hq), F32))
        for j in range(hz):
            zz = half * hz + j
            dq_snd[zz] = (dq[:, j * HEAD : (j + 1) * HEAD] * factor).astype(BF)

            @pl.when(zz != z)
            def _():
                z_give(4, dq_snd, dq_rcv, zz).start()

    backward(far, True)
    backward(near, False)

    full = jnp.zeros((HEAD, HEAD), F32)
    for d in order:
        z_give_arrival(1, o_rcv, d)
    for zz in range(nz):
        full = full + ld[z, 8 + zz : 9 + zz, :] * o_rcv[zz].astype(F32)
    att_all[0] = (full / ld[z, 2:3, :]).T.astype(BF)
    for i in range(1, 4):
        go(remote(att_all.at[0], att_all.at[i], cs.at[1, i], cr.at[1, i], to_cols[i]))

    def dp_rows(rr):
        return pl.ds(pl.multiple_of(rr * HEAD, HEAD), HEAD)

    mine, theirs, both = dp_rows(r), dp_rows(1 - r), slice(0, 2 * HEAD)

    def dkv_arrival(yy, rr):
        ref = dkv_rcv.at[half_rows(yy, rr)]
        remote(ref, ref, ds.at[0, 0], dr.at[2 * yy + rr], to_row).wait_recv()
        dkv_own[half_rows(y, r), :] += dkv_rcv[half_rows(yy, rr), :].astype(F32)

    for d in range(1, ny):

        @pl.when(y + d < ny)
        def _():
            dkv_arrival(wrap(y + d, ny), r)
            dkv_arrival(wrap(y + d, ny), 1 - r)

    dkv_arrival(y, 1 - r)
    dp_all[0, mine, HEAD:] = dkv_own[half_rows(y, r), :].astype(BF)

    peers = [to_cols[2], to_diag, to_row]
    slots = [(2, r), (2, 1 - r), (0, 1 - r)]
    lanes_of_part = [pl.ds(HEAD, 2 * HEAD), pl.ds(0, HEAD)]

    def dp_ref(col, rr, part):
        return dp_all.at[col, dp_rows(rr), lanes_of_part[part]]

    def dp_copy(i, part):
        return remote(
            dp_ref(0, r, part),
            dp_ref((2, 2, 0, 1)[i], r, part),
            gs.at[part, i],
            gr.at[part, i],
            to_cols[1] if i == 3 else peers[i],
        )

    def dp_relay(i, part):
        col, rr = slots[i]
        return remote(
            dp_ref(col, rr, part),
            dp_ref(col + 1, rr, part),
            gs.at[part, 4 + i],
            gr.at[part, 4 + i],
            to_cols[1],
        )

    def dp_arrival(i, part):
        col, rr = (1, r) if i == 3 else slots[i % 4]
        ref = dp_ref(col + 1 if i > 3 else col, rr, part)
        remote(ref, ref, gs.at[part, i], gr.at[part, i], to_cols[1]).wait_recv()

    for i in range(4):
        go(dp_copy(i, 0))
    for i in range(1, 4):
        remote(att_all.at[i], att_all.at[i], cs.at[1, i], cr.at[1, i], to_cols[i]).wait_recv()
    for j in range(4):
        part = width // 4
        lanes = pl.ds(j * part, part)
        total_out = jnp.dot(att_all[0], wo_v[0, :, lanes], preferred_element_type=F32)
        for i in range(1, 4):
            total_out = total_out + jnp.dot(
                att_all[i], wo_v[i, :, lanes], preferred_element_type=F32
            )
        out_ref[:, lanes] = total_out.astype(BF)
    dq_sum = dq_snd[z].astype(F32)
    for d in order:
        z_give_arrival(4, dq_rcv, d)
        dq_sum = dq_sum + dq_rcv[wrap(z - d, nz)].astype(F32)
    dp_all[0, mine, :HEAD] = dq_sum.T.astype(BF)
    for i in range(4):
        go(dp_copy(i, 1))

    for t in range(2, yl + 1):
        for round_columns in columns:
            for column in round_columns:
                y_round(*w_column(*column), t)
    sib_w.wait_recv()

    blk = min(512, depth)

    def dx_add(i, rows, first=False, last=False):
        def turn(j, carry):
            start = pl.multiple_of(j * blk, blk)
            out = pl.ds(start, blk)
            weight = wv[pl.ds(c * depth + start, blk), :] if i == 0 else w_x[i - 1, out, :]
            acc = dot_nt(dp_all[i, rows, :], weight)
            if not first:
                acc = acc + dx_acc[rows, out]
            if last:
                dx_ref[rows, out] = acc.astype(BF)
            else:
                dx_acc[rows, out] = acc
            return carry

        lax.fori_loop(0, depth // blk, turn, 0)

    dx_add(0, mine, first=True)
    dp_arrival(3, 0)
    dp_arrival(3, 1)
    dx_add(1, mine)
    for part in range(2):
        for i in range(3):
            dp_arrival(i, part)
            go(dp_relay(i, part))
    dx_add(0, theirs, first=True)
    dx_add(2, both)
    for part in range(2):
        dp_arrival(6, part)
    dx_add(1, theirs)
    for part in range(2):
        dp_arrival(4, part)
        dp_arrival(5, part)
    dx_add(3, both, last=True)

    for d in range(1, ny):

        @pl.when(y + d < ny)
        def _():
            for k in range(hk):
                kv_send(d, 0, k).wait_send()
                kv_send(d, 1, k).wait_send()

    def sent_turn(yy, carry):
        dkv_send(yy, 1 - r).wait_send()

        @pl.when(yy < y)
        def _():
            dkv_send(yy, r).wait_send()

        return carry

    lax.fori_loop(0, y + 1, sent_turn, 0)
    for d in order:
        to = wrap(z + d, nz)
        z_give(1, o_snd, o_rcv, to).wait_send()
        st_copy(to).wait_send()
        z_give(4, dq_snd, dq_rcv, to).wait_send()
    for copy in seeds + [sib_w, sib_wo] + started:
        copy.wait_send()
    for k in range(CHUNKS):
        token_copy(0, k).wait_send()
        token_copy(1, k).wait_send()


def body(nz, tokens, input_weight, output_weight, output_cotangent):
    ny = lax.axis_size("seq") // nz
    rows, depth = tokens.shape
    n = input_weight.shape[1]
    width = output_cotangent.shape[1]
    hbm = pl.BlockSpec(memory_space=pl.ANY)
    vm = pl.BlockSpec(memory_space=pltpu.VMEM)
    nk, nq = ny * 2 * HEAD, nz * HEAD
    V = pltpu.VMEM
    sem = pltpu.SemaphoreType.DMA
    zl, zsh = ring(nz)
    yl, ysh = ring(ny)
    return pl.pallas_call(
        functools.partial(layer_kernel, ny, nz),
        out_shape=(
            jax.ShapeDtypeStruct(output_cotangent.shape, BF),
            jax.ShapeDtypeStruct(tokens.shape, BF),
        ),
        in_specs=[hbm] * 4,
        out_specs=(vm, vm),
        scratch_shapes=[
            V((4, rows, depth), BF),
            V((4 * depth, n), BF),
            V((HEAD, n), F32),
            V((HEAD, n), F32),
            V((3, depth, n), BF),
            V((4, HEAD, width), BF),
            V((nq, HEAD), BF),
            V((nk, 2 * HEAD), BF),
            V((nq, HEAD), BF),
            V((HEAD, width), BF),
            V((4, HEAD, HEAD), F32),
            V((4, HEAD, HEAD), F32),
            V((HEAD, HEAD), F32),
            V((nk, nq), F32),
            V((nz, HEAD, HEAD), BF),
            V((nz, HEAD, HEAD), BF),
            V((3, nz, HEAD), F32),
            V((nz, 3, nz, HEAD), F32),
            V((8, nq), F32),
            V((HEAD, nq), F32),
            V((nz, nz, HEAD), F32),
            V((nz, 16, HEAD), F32),
            V((4, HEAD, HEAD), BF),
            V((nz, HEAD, HEAD), BF),
            V((nz, HEAD, HEAD), BF),
            V((nk, 2 * HEAD), F32),
            V((nk, 2 * HEAD), BF),
            V((nk, 2 * HEAD), BF),
            V((4, 2 * HEAD, n), BF),
            V(tokens.shape, F32),
            sem((4,)),
            sem((3, 2)),
            sem((3, 2)),
            sem((2, zl + 1)),
            sem((2, zl + 1)),
            sem((nz, 2, yl + 1)),
            sem((nz, 2, yl + 1)),
            sem((2, zl + 1)),
            sem((2, zl + 1)),
            sem((2,)),
            sem((2,)),
            sem((3, CHUNKS)),
            sem((3, CHUNKS)),
            sem((CHUNKS // 2,)),
            sem((CHUNKS // 2,)),
            sem((CHUNKS // 2, nz)),
            sem((CHUNKS // 2, nz)),
            sem((5, nz)),
            sem((5, nz)),
            sem((CHUNKS // 2, 2 * ny + 1)),
            sem((CHUNKS // 2, 2 * ny + 1)),
            sem((2, 4)),
            sem((2, 4)),
            sem((ny, 2)),
            sem((2 * ny,)),
            sem((2, 7)),
            sem((2, 7)),
        ],
        compiler_params=pltpu.CompilerParams(
            collective_id=0, has_side_effects=True, vmem_limit_bytes=52 * 2**20
        ),
        cost_estimate=pl.CostEstimate(
            flops=6_000_000_000, bytes_accessed=20_000_000, transcendentals=2_000_000
        ),
        name="layer",
    )(tokens, input_weight, output_weight, output_cotangent)


def solution(mesh):
    seq = mesh.shape["seq"]
    nz = 8 if seq % 32 == 0 else seq // 2
    return jax.shard_map(
        functools.partial(body, nz),
        mesh=mesh,
        in_specs=(
            P("seq", ("row", "col")),
            P("row", "col"),
            P("col", None),
            P(("seq", "row"), "col"),
        ),
        out_specs=(P(("seq", "row"), "col"), P("seq", ("row", "col"))),
        check_vma=False,
    )
```

```python
import functools
import math

import jax
import jax.numpy as jnp
from jax import lax
from jax.experimental import pallas as pl
from jax.experimental.pallas import tpu as pltpu
from jax.sharding import PartitionSpec as P

HEAD = 128
MESH = pl.DeviceIdType.MESH
masked_score = -1e30
BF = jnp.bfloat16
F32 = jnp.float32
CHUNKS = 4
AHEAD = 2


def remote(src, dst, send_sem, recv_sem, device):
    return pltpu.make_async_remote_copy(
        src_ref=src,
        dst_ref=dst,
        send_sem=send_sem,
        recv_sem=recv_sem,
        device_id=device,
        device_id_type=MESH,
    )


def greet(devices):
    barrier = pltpu.get_barrier_semaphore()
    for device in devices:
        pl.semaphore_signal(barrier, inc=1, device_id=device, device_id_type=MESH)
    pl.semaphore_wait(barrier, len(devices))


def dot_nt(a, b):
    return lax.dot_general(a, b, (((1,), (1,)), ((), ())), preferred_element_type=F32)


def dot_tn(a, b):
    return lax.dot_general(a, b, (((0,), (0,)), ((), ())), preferred_element_type=F32)


def flip(c, bits):
    low, high = lax.rem(c, 2), c // 2
    if bits & 1:
        low = 1 - low
    if bits & 2:
        high = 1 - high
    return high * 2 + low


def ring(size):
    return size // 2, (size - 1) // 2


def layer_kernel(
    ny,
    nz,
    t_ref,
    w_ref,
    wo_ref,
    do_ref,
    out_ref,
    dx_ref,
    tbuf,
    wv,
    psend,
    precv,
    w_x,
    wo_v,
    q_all,
    kv_all,
    u_all,
    do_v,
    ups,
    upr,
    up_own,
    s_all,
    pg_all,
    o_snd,
    o_rcv,
    st_snd,
    st_rcv,
    st_rows,
    o_all,
    o_scale,
    ld,
    att_all,
    dq_snd,
    dq_rcv,
    dkv_own,
    dkv_snd,
    dkv_rcv,
    dp_all,
    dx_acc,
    lsem,
    sds,
    sdr,
    wzs,
    wzr,
    wys,
    wyr,
    ozs,
    ozr,
    sbs,
    sbr,
    tks,
    tkr,
    pts,
    ptr,
    qs,
    qr,
    zs,
    zr,
    kvs,
    kvr,
    cs,
    cr,
    ds,
    dr,
    gs,
    gr,
):
    s, r, c = lax.axis_index("seq"), lax.axis_index("row"), lax.axis_index("col")
    y, z = s // nz, lax.rem(s, nz)
    core = lax.rem(c, 2)
    sgn = 1 - 2 * core
    factor = 1.0 / math.sqrt(HEAD)
    depth = t_ref.shape[1]
    width = do_ref.shape[1]
    step = 2 * HEAD // CHUNKS
    hk = CHUNKS // 2
    slab = 2 * HEAD
    cols = [c, flip(c, 1), flip(c, 2), flip(c, 3)]
    to_cols = [(s, r, p) for p in cols]
    to_row = (s, 1 - r, c)
    to_diag = (s, 1 - r, cols[2])

    def wrap(a, n):
        return lax.rem(a + 2 * n, n)

    def dev_z(zz):
        return (y * nz + zz, r, c)

    def dev_y(yy):
        return (yy * nz + z, r, c)

    own_tokens = pltpu.make_async_copy(t_ref, tbuf.at[0], lsem.at[0])
    own_w = pltpu.make_async_copy(w_ref, wv, lsem.at[1])
    own_wo = pltpu.make_async_copy(
        wo_ref.at[:, pl.ds(pl.multiple_of(c * width, 128), width)], wo_v.at[0], lsem.at[2]
    )
    own_do = pltpu.make_async_copy(do_ref, do_v, lsem.at[3])
    own_tokens.start()
    own_w.start()
    own_wo.start()
    own_do.start()
    greet(
        [dev_z(wrap(z + d, nz)) for d in range(1, nz)]
        + [dev_y(wrap(y + d, ny)) for d in range(1, ny)]
        + [(wrap(y + d, ny) * nz + z, 1 - r, c) for d in range(1, ny)]
        + [to_row]
        + to_cols[1:]
        + [to_diag, (s, 1 - r, cols[3])]
    )

    piece = depth // (ny * nz)
    orow = HEAD // nz
    half_width = width // 2

    def w_piece(yy, zz):
        start = pl.multiple_of((yy * nz + zz) * piece, 16)
        return w_x.at[pl.ds(1, 2), pl.ds(start, piece), :]

    def o_piece(zz):
        rows = pl.ds(pl.multiple_of(zz * orow, 16), orow)
        return wo_v.at[pl.ds(2, 2), rows, pl.ds(0, half_width)]

    w_seeds, o_seeds, o_direct = [], [], []
    for h in range(2):
        p = cols[2 + h]
        start = pl.multiple_of(s * piece, 16)
        w_seeds.append(
            remote(
                w_ref.at[pl.ds(pl.multiple_of(p * depth + s * piece, 16), piece), :],
                w_x.at[1 + h, pl.ds(start, piece), :],
                sds.at[0, h],
                sdr.at[0, h],
                to_cols[2 + h],
            )
        )
        orows = pl.ds(pl.multiple_of(z * orow, 16), orow)
        o_seeds.append(
            remote(
                wo_ref.at[orows, pl.ds(pl.multiple_of(p * width, 128), half_width)],
                wo_v.at[2 + h, orows, pl.ds(0, half_width)],
                sds.at[1, h],
                sdr.at[1, h],
                (s, 1 - r, p),
            )
        )
        o_direct.append(
            remote(
                wo_ref.at[:, pl.ds(pl.multiple_of(p * width + half_width, 128), half_width)],
                wo_v.at[2 + h, :, pl.ds(half_width, half_width)],
                sds.at[2, h],
                sdr.at[2, h],
                (s, 1 - r, p),
            )
        )
    seeds = w_seeds + o_seeds + o_direct
    for copy in w_seeds + o_seeds + o_direct:
        copy.start()

    def rows_of(k):
        start = (1 - r) * HEAD + k * step if k < hk else r * HEAD + (k - hk) * step
        return pl.ds(pl.multiple_of(start, step), step)

    def token_copy(kind, k):
        rows = rows_of(k)
        if kind == 0:
            return remote(
                t_ref.at[rows], tbuf.at[2, rows], tks.at[0, k], tkr.at[0, k], to_cols[2]
            )
        if kind == 1:
            return remote(
                t_ref.at[rows], tbuf.at[1, rows], tks.at[1, k], tkr.at[1, k], to_cols[1]
            )
        return remote(
            tbuf.at[2, rows], tbuf.at[3, rows], tks.at[2, k], tkr.at[2, k], to_cols[1]
        )

    for k in range(AHEAD):
        token_copy(0, k).start()
    for k in range(CHUNKS):
        token_copy(1, k).start()
    sib_w = remote(
        w_ref.at[pl.ds(pl.multiple_of(cols[1] * depth, 16), depth), :],
        w_x.at[0],
        sbs.at[0],
        sbr.at[0],
        to_cols[1],
    )
    sib_wo = remote(
        wo_ref.at[:, pl.ds(pl.multiple_of(cols[1] * width, 128), width)],
        wo_v.at[1],
        sbs.at[1],
        sbr.at[1],
        to_cols[1],
    )
    sib_wo.start()
    sib_w.start()

    zl, zsh = ring(nz)
    yl, ysh = ring(ny)
    z_next, z_prev = wrap(z + sgn, nz), wrap(z - sgn, nz)
    y_next, y_prev = wrap(y + sgn, ny), wrap(y - sgn, ny)

    def zq(long, t):
        return wrap(z - sgn * t, nz) if long else wrap(z + sgn * t, nz)

    def yq(long, t):
        return wrap(y - sgn * t, ny) if long else wrap(y + sgn * t, ny)

    def z_ring(pick, snd, rcv, long, t):
        ref = pick(zq(long, t))
        way = 0 if long else 1
        return remote(
            ref, ref, snd.at[way, t], rcv.at[way, t + 1], dev_z(z_next if long else z_prev)
        )

    def z_ring_in(pick, snd, rcv, long, t):
        ref = pick(zq(long, t))
        way = 0 if long else 1
        return remote(ref, ref, snd.at[way, t], rcv.at[way, t], dev_z(z_next))

    def y_ring(pick, snd, rcv, long, t):
        ref = pick(yq(long, t))
        way = 0 if long else 1
        return remote(
            ref, ref, snd.at[way, t], rcv.at[way, t + 1], dev_y(y_next if long else y_prev)
        )

    def y_ring_in(pick, snd, rcv, long, t):
        ref = pick(yq(long, t))
        way = 0 if long else 1
        return remote(ref, ref, snd.at[way, t], rcv.at[way, t], dev_y(y_next))

    started = []

    def go(copy):
        copy.start()
        started.append(copy)

    def w_here(zz):
        return w_piece(y, zz)

    def z_start(pick, snd, rcv):
        if zl:
            go(z_ring(pick, snd, rcv, True, 0))
        if zsh:
            go(z_ring(pick, snd, rcv, False, 0))

    def y_start(pick, snd, rcv):
        if yl:
            go(y_ring(pick, snd, rcv, True, 0))
        if ysh:
            go(y_ring(pick, snd, rcv, False, 0))

    def z_round(pick, snd, rcv, t):
        ways = []
        for long, hops in ((True, zl), (False, zsh)):
            if t <= hops:
                z_ring_in(pick, snd, rcv, long, t).wait_recv()
                if t < hops:
                    go(z_ring(pick, snd, rcv, long, t))
                ways.append(long)
        return ways

    def y_round(pick, snd, rcv, t):
        for long, hops in ((True, yl), (False, ysh)):
            if t <= hops:
                y_ring_in(pick, snd, rcv, long, t).wait_recv()
                if t < hops:
                    go(y_ring(pick, snd, rcv, long, t))

    def w_column(long, t):
        zz = zq(long, t)
        index = t if long else zl + t

        def pick(yy):
            return w_piece(yy, zz)

        return pick, wys.at[index], wyr.at[index]

    def product(i, rows, start):
        return jnp.dot(
            tbuf[i, rows, :],
            wv[pl.ds(pl.multiple_of(start, 16), depth), :],
            preferred_element_type=F32,
        )

    def part_copy(k):
        rows = pl.ds(k * step, step)
        return remote(psend.at[rows], precv.at[rows], pts.at[k], ptr.at[k], to_row)

    def z_rows(zz):
        return pl.ds(pl.multiple_of(zz * HEAD, HEAD), HEAD)

    def q_rows(zz, k):
        return pl.ds(pl.multiple_of(zz * HEAD + k * step, step), step)

    def kv_rows(yy, rr, k):
        return pl.ds(pl.multiple_of(yy * slab + rr * HEAD + k * step, step), step)

    def token_arrival(kind, k):
        ref = tbuf.at[(2, 1, 3)[kind], rows_of(k)]
        remote(ref, ref, tks.at[kind, k], tkr.at[kind, k], to_cols[1]).wait_recv()

    def project_relay(k):
        token_arrival(0, k)
        go(token_copy(2, k))

    def project(k):
        rows = rows_of(k)
        token_arrival(1, k)
        acc = product(0, rows, c * depth) + product(1, rows, cols[1] * depth)
        acc = acc + product(2, rows, cols[2] * depth)
        token_arrival(2, k)
        acc = acc + product(3, rows, cols[3] * depth)
        if k < hk:
            psend[pl.ds(k * step, step), :] = acc
            go(part_copy(k))
        else:
            part_copy(k - hk).wait_recv()
            out = pl.ds((k - hk) * step, step)
            packed = (acc + precv[out, :]).astype(BF)
            q_all[q_rows(z, k - hk), :] = packed[:, :HEAD]
            kv_all[kv_rows(y, r, k - hk), :] = packed[:, HEAD:]

    def kv_row(k):
        rows = kv_rows(y, r, k)
        return remote(kv_all.at[rows], kv_all.at[rows], kvs.at[k, 0], kvr.at[k, 2 * ny], to_row)

    def kv_row_arrival(k):
        rows = kv_rows(y, 1 - r, k)
        return remote(kv_all.at[rows], kv_all.at[rows], kvs.at[k, 0], kvr.at[k, 2 * ny], to_row)

    def kv_send(d, other, k):
        rr = 1 - r if other else r
        rows = kv_rows(y, rr, k)
        return remote(
            kv_all.at[rows],
            kv_all.at[rows],
            kvs.at[k, 1 + 2 * d + other],
            kvr.at[k, 2 * y + other],
            dev_y(wrap(y + d, ny)),
        )

    def kv_arrival(yy, other, k):
        rr = 1 - r if other else r
        rows = kv_rows(yy, rr, k)
        return remote(
            kv_all.at[rows], kv_all.at[rows], kvs.at[k, 0], kvr.at[k, 2 * yy + other], to_row
        )

    def kv_sends(other, k):
        for d in range(1, ny):

            @pl.when(y + d < ny)
            def _():
                kv_send(d, other, k).start()

    def q_send(d, k):
        rows = q_rows(z, k)
        to = wrap(z + d, nz)
        return remote(q_all.at[rows], q_all.at[rows], qs.at[k, d], qr.at[k, d], dev_z(to))

    def q_arrival(d, k):
        rows = q_rows(wrap(z - d, nz), k)
        return remote(q_all.at[rows], q_all.at[rows], qs.at[k, d], qr.at[k, d], dev_z(z_next))

    order = sorted(range(1, nz), key=lambda d: -min(d, nz - d))

    def share(k):
        go(kv_row(k))
        kv_sends(0, k)
        for d in order:
            go(q_send(d, k))

    def upstream_terms():
        own_do.wait()
        own_wo.wait()
        for copy in o_direct:
            copy.wait_recv()
        for i in (2, 3):
            ups[i] = dot_nt(do_v[...], wo_v[i])
            go(remote(ups.at[i], upr.at[i], cs.at[0, i], cr.at[0, i], to_cols[i]))
        sib_wo.wait_recv()
        ups[1] = dot_nt(do_v[...], wo_v[1])
        go(remote(ups.at[1], upr.at[1], cs.at[0, 1], cr.at[0, 1], to_cols[1]))
        up_own[...] = dot_nt(do_v[...], wo_v[0])

    for copy in w_seeds:
        copy.wait_recv()
    z_start(w_here, wzs, wzr)
    pick, snd, rcv = w_column(True, 0)
    y_start(pick, snd, rcv)
    for copy in o_seeds:
        copy.wait_recv()
    z_start(o_piece, ozs, ozr)
    columns = [[(True, 0)]]
    own_tokens.wait()
    own_w.wait()
    for k in range(max(CHUNKS, zl)):
        t = k + 1
        if t <= zl:
            ways = z_round(w_here, wzs, wzr, t)
            for long in ways:
                y_start(*w_column(long, t))
            columns.append([(long, t) for long in ways])
            for column in columns[t - 1]:
                y_round(*w_column(*column), 1)
            z_round(o_piece, ozs, ozr, t)
        if k < CHUNKS:
            project_relay(k)
            if k + AHEAD < CHUNKS:
                token_copy(0, k + AHEAD).start()
            if k == CHUNKS - 1:
                upstream_terms()
            project(k)
        if hk <= k < CHUNKS:
            share(k - hk)

    for k in range(hk):
        kv_row_arrival(k).wait_recv()
        kv_sends(1, k)

    for i in range(1, 4):
        remote(upr.at[i], upr.at[i], cs.at[0, i], cr.at[0, i], to_cols[i]).wait_recv()
    up = up_own[...]
    for i in range(1, 4):
        up = up + upr[i]
    u_all[z_rows(z), :] = up.astype(BF)
    for d in order:
        to = wrap(z + d, nz)
        rows = z_rows(z)
        go(remote(u_all.at[rows], u_all.at[rows], zs.at[0, to], zr.at[0, z], dev_z(to)))
    for column in columns[zl]:
        y_round(*w_column(*column), 1)

    for d in order:
        for k in range(hk):
            q_arrival(d, k).wait_recv()
    hz = nz // 2
    hq = hz * HEAD
    near = z // hz
    far = 1 - near
    lane = lax.broadcasted_iota(jnp.int32, (1, hq), 1)
    kofs = lax.broadcasted_iota(jnp.int32, (slab, 1), 0)

    def y_rows(yy):
        return pl.ds(pl.multiple_of(yy * slab, slab), slab)

    def q_half(half):
        return pl.ds(pl.multiple_of(half * hq, hq), hq)

    def z_give(kind, src, dst, to):
        return remote(src.at[to], dst.at[z], zs.at[kind, to], zr.at[kind, z], dev_z(to))

    def z_give_arrival(kind, dst, d):
        slot = wrap(z - d, nz)
        remote(
            dst.at[slot], dst.at[slot], zs.at[kind, slot], zr.at[kind, slot], dev_z(z_next)
        ).wait_recv()

    def score(half, first):
        lanes_of = q_half(half)
        queries = q_all[lanes_of, :]
        qpos = (y * nz + half * hz + lane // HEAD) * slab + r * HEAD + lane % HEAD

        def score_turn(yy, largest):
            if first:

                @pl.when(yy < y)
                def _():
                    for k in range(hk):
                        kv_arrival(yy, 0, k).wait_recv()
                        kv_arrival(yy, 1, k).wait_recv()

            keys = kv_all[y_rows(yy), :HEAD]
            scores = dot_nt(keys, queries) * factor
            kpos = (yy * nz + z) * slab + kofs
            scores = jnp.where(kpos <= qpos, scores, masked_score)
            s_all[y_rows(yy), lanes_of] = scores
            return jnp.maximum(largest, jnp.max(scores, axis=0, keepdims=True))

        return lax.fori_loop(0, y + 1, score_turn, jnp.full((1, hq), masked_score, F32))

    def weigh(half, largest):
        lanes_of = q_half(half)

        def weight_turn(yy, carry):
            total, mixed = carry
            weights = jnp.exp(s_all[y_rows(yy), lanes_of] - largest)
            total = total + jnp.sum(weights, axis=0, keepdims=True)
            mixed = mixed + dot_tn(kv_all[y_rows(yy), HEAD:], weights.astype(BF))
            return total, mixed

        total, mixed = lax.fori_loop(
            0, y + 1, weight_turn, (jnp.zeros((1, hq), F32), jnp.zeros((HEAD, hq), F32))
        )
        st_rows[0:1, lanes_of] = largest
        st_rows[1:2, lanes_of] = total
        o_all[:, lanes_of] = mixed

    top_far = score(far, True)
    top_near = score(near, False)

    weigh(far, top_far)
    weigh(near, top_near)

    for zz in range(nz):
        lanes = slice(zz * HEAD, (zz + 1) * HEAD)
        o_snd[zz] = o_all[:, lanes].astype(BF)
        st_snd[0, zz : zz + 1, :] = st_rows[0:1, lanes]
        st_snd[1, zz : zz + 1, :] = st_rows[1:2, lanes]
    for d in order:
        slot = wrap(z - d, nz)
        ref = u_all.at[z_rows(slot)]
        remote(ref, ref, zs.at[0, slot], zr.at[0, slot], dev_z(z_next)).wait_recv()
    for zz in range(nz):
        lanes = slice(zz * HEAD, (zz + 1) * HEAD)
        up_t = u_all[lanes, :].astype(F32).T
        st_snd[2, zz : zz + 1, :] = jnp.sum(up_t * o_all[:, lanes], axis=0, keepdims=True)

    def st_copy(to):
        return remote(st_snd, st_rcv.at[z], zs.at[2, to], zr.at[2, z], dev_z(to))

    for d in order:
        st_copy(wrap(z + d, nz)).start()
    for d in order:
        z_give(1, o_snd, o_rcv, wrap(z + d, nz)).start()
    o_rcv[z] = o_snd[z]
    st_rcv[z] = st_snd[...]

    def ahead_turn(yy, carry):
        for half in range(2):
            lanes = slice(half * hq, (half + 1) * hq)
            pg_all[y_rows(yy), lanes] = dot_nt(kv_all[y_rows(yy), HEAD:], u_all[lanes, :])
            s_all[y_rows(yy), lanes] = jnp.exp(s_all[y_rows(yy), lanes] - st_rows[0:1, lanes])
        return carry

    lax.fori_loop(0, y + 1, ahead_turn, 0)
    for d in order:
        z_give_arrival(2, st_rcv, d)
    top = st_rcv[0, 0]
    for zz in range(1, nz):
        top = jnp.maximum(top, st_rcv[zz, 0])
    full_total = jnp.zeros((nz, HEAD), F32)
    full_delta = jnp.zeros((nz, HEAD), F32)
    for zz in range(nz):
        scale = jnp.exp(st_rcv[zz, 0] - top)
        full_total = full_total + scale * st_rcv[zz, 1]
        full_delta = full_delta + scale * st_rcv[zz, 2]
        o_scale[zz] = scale
    all_logsum = top + jnp.log(full_total)
    all_delta = full_delta / full_total
    for zz in range(nz):
        row = slice(zz, zz + 1)
        ld[zz, 0:1, :] = all_logsum[row]
        ld[zz, 1:2, :] = all_delta[row]
        ld[zz, 2:3, :] = full_total[row]
        for other in range(nz):
            ld[zz, 8 + other : 9 + other, :] = o_scale[other, row, :]

    def half_rows(yy, rr):
        return pl.ds(pl.multiple_of(yy * slab + rr * HEAD, HEAD), HEAD)

    def dkv_send(yy, rr):
        return remote(
            dkv_snd.at[half_rows(yy, rr)],
            dkv_rcv.at[half_rows(y, r)],
            ds.at[yy, rr],
            dr.at[2 * y + r],
            (yy * nz + z, rr, c),
        )

    def backward(half, first):
        lanes_of = q_half(half)
        queries, upstream = q_all[lanes_of, :], u_all[lanes_of, :]
        logsum = jnp.concatenate([ld[half * hz + j, 0:1, :] for j in range(hz)], axis=1)
        scale = jnp.exp(st_rows[0:1, lanes_of] - logsum)
        delta = jnp.concatenate([ld[half * hz + j, 1:2, :] for j in range(hz)], axis=1)

        def grad_turn(yy, dq):
            keys = kv_all[y_rows(yy), :HEAD]
            probs = s_all[y_rows(yy), lanes_of] * scale
            score_grad = (probs * (pg_all[y_rows(yy), lanes_of] - delta)).astype(BF)
            dk = jnp.dot(score_grad, queries, preferred_element_type=F32) * factor
            dv = jnp.dot(probs.astype(BF), upstream, preferred_element_type=F32)
            if first:
                dkv_own[y_rows(yy), :HEAD] = dk
                dkv_own[y_rows(yy), HEAD:] = dv
            else:
                dk = dk + dkv_own[y_rows(yy), :HEAD]
                dv = dv + dkv_own[y_rows(yy), HEAD:]
                dkv_snd[y_rows(yy), :HEAD] = dk.astype(BF)
                dkv_snd[y_rows(yy), HEAD:] = dv.astype(BF)

                @pl.when(yy < y)
                def _():
                    dkv_send(yy, r).start()

                dkv_send(yy, 1 - r).start()

                @pl.when(yy == y)
                def _():
                    dkv_own[y_rows(yy), :HEAD] = dk
                    dkv_own[y_rows(yy), HEAD:] = dv

            return dq + dot_tn(keys, score_grad)

        dq = lax.fori_loop(0, y + 1, grad_turn, jnp.zeros((HEAD, hq), F32))
        for j in range(hz):
            zz = half * hz + j
            dq_snd[zz] = (dq[:, j * HEAD : (j + 1) * HEAD] * factor).astype(BF)

            @pl.when(zz != z)
            def _():
                z_give(4, dq_snd, dq_rcv, zz).start()

    backward(far, True)
    backward(near, False)

    full = jnp.zeros((HEAD, HEAD), F32)
    for d in order:
        z_give_arrival(1, o_rcv, d)
    for zz in range(nz):
        full = full + ld[z, 8 + zz : 9 + zz, :] * o_rcv[zz].astype(F32)
    att_all[0] = (full / ld[z, 2:3, :]).T.astype(BF)
    for i in range(1, 4):
        go(remote(att_all.at[0], att_all.at[i], cs.at[1, i], cr.at[1, i], to_cols[i]))

    def dp_rows(rr):
        return pl.ds(pl.multiple_of(rr * HEAD, HEAD), HEAD)

    mine, theirs, both = dp_rows(r), dp_rows(1 - r), slice(0, 2 * HEAD)

    def dkv_arrival(yy, rr):
        ref = dkv_rcv.at[half_rows(yy, rr)]
        remote(ref, ref, ds.at[0, 0], dr.at[2 * yy + rr], to_row).wait_recv()
        dkv_own[half_rows(y, r), :] += dkv_rcv[half_rows(yy, rr), :].astype(F32)

    for d in range(1, ny):

        @pl.when(y + d < ny)
        def _():
            dkv_arrival(wrap(y + d, ny), r)
            dkv_arrival(wrap(y + d, ny), 1 - r)

    dkv_arrival(y, 1 - r)
    dp_all[0, mine, HEAD:] = dkv_own[half_rows(y, r), :].astype(BF)

    peers = [to_cols[2], to_diag, to_row]
    slots = [(2, r), (2, 1 - r), (0, 1 - r)]
    lanes_of_part = [pl.ds(HEAD, 2 * HEAD), pl.ds(0, HEAD)]

    def dp_ref(col, rr, part):
        return dp_all.at[col, dp_rows(rr), lanes_of_part[part]]

    def dp_copy(i, part):
        return remote(
            dp_ref(0, r, part),
            dp_ref((2, 2, 0, 1)[i], r, part),
            gs.at[part, i],
            gr.at[part, i],
            to_cols[1] if i == 3 else peers[i],
        )

    def dp_relay(i, part):
        col, rr = slots[i]
        return remote(
            dp_ref(col, rr, part),
            dp_ref(col + 1, rr, part),
            gs.at[part, 4 + i],
            gr.at[part, 4 + i],
            to_cols[1],
        )

    def dp_arrival(i, part):
        col, rr = (1, r) if i == 3 else slots[i % 4]
        ref = dp_ref(col + 1 if i > 3 else col, rr, part)
        remote(ref, ref, gs.at[part, i], gr.at[part, i], to_cols[1]).wait_recv()

    for i in range(4):
        go(dp_copy(i, 0))
    for i in range(1, 4):
        remote(att_all.at[i], att_all.at[i], cs.at[1, i], cr.at[1, i], to_cols[i]).wait_recv()
    for j in range(4):
        part = width // 4
        lanes = pl.ds(j * part, part)
        total_out = jnp.dot(att_all[0], wo_v[0, :, lanes], preferred_element_type=F32)
        for i in range(1, 4):
            total_out = total_out + jnp.dot(
                att_all[i], wo_v[i, :, lanes], preferred_element_type=F32
            )
        out_ref[:, lanes] = total_out.astype(BF)
    dq_sum = dq_snd[z].astype(F32)
    for d in order:
        z_give_arrival(4, dq_rcv, d)
        dq_sum = dq_sum + dq_rcv[wrap(z - d, nz)].astype(F32)
    dp_all[0, mine, :HEAD] = dq_sum.T.astype(BF)
    for i in range(4):
        go(dp_copy(i, 1))

    for t in range(2, yl + 1):
        for round_columns in columns:
            for column in round_columns:
                y_round(*w_column(*column), t)
    sib_w.wait_recv()

    blk = min(512, depth)

    def dx_add(i, rows, first=False, last=False):
        def turn(j, carry):
            start = pl.multiple_of(j * blk, blk)
            out = pl.ds(start, blk)
            weight = wv[pl.ds(c * depth + start, blk), :] if i == 0 else w_x[i - 1, out, :]
            acc = dot_nt(dp_all[i, rows, :], weight)
            if not first:
                acc = acc + dx_acc[rows, out]
            if last:
                dx_ref[rows, out] = acc.astype(BF)
            else:
                dx_acc[rows, out] = acc
            return carry

        lax.fori_loop(0, depth // blk, turn, 0)

    dx_add(0, mine, first=True)
    dp_arrival(3, 0)
    dp_arrival(3, 1)
    dx_add(1, mine)
    for part in range(2):
        for i in range(3):
            dp_arrival(i, part)
            go(dp_relay(i, part))
    dx_add(0, theirs, first=True)
    dx_add(2, both)
    for part in range(2):
        dp_arrival(6, part)
    dx_add(1, theirs)
    for part in range(2):
        dp_arrival(4, part)
        dp_arrival(5, part)
    dx_add(3, both, last=True)

    for d in range(1, ny):

        @pl.when(y + d < ny)
        def _():
            for k in range(hk):
                kv_send(d, 0, k).wait_send()
                kv_send(d, 1, k).wait_send()

    def sent_turn(yy, carry):
        dkv_send(yy, 1 - r).wait_send()

        @pl.when(yy < y)
        def _():
            dkv_send(yy, r).wait_send()

        return carry

    lax.fori_loop(0, y + 1, sent_turn, 0)
    for d in order:
        to = wrap(z + d, nz)
        z_give(1, o_snd, o_rcv, to).wait_send()
        st_copy(to).wait_send()
        z_give(4, dq_snd, dq_rcv, to).wait_send()
    for copy in seeds + [sib_w, sib_wo] + started:
        copy.wait_send()
    for k in range(CHUNKS):
        token_copy(0, k).wait_send()
        token_copy(1, k).wait_send()


def body(nz, tokens, input_weight, output_weight, output_cotangent):
    ny = lax.axis_size("seq") // nz
    rows, depth = tokens.shape
    n = input_weight.shape[1]
    width = output_cotangent.shape[1]
    hbm = pl.BlockSpec(memory_space=pl.ANY)
    vm = pl.BlockSpec(memory_space=pltpu.VMEM)
    nk, nq = ny * 2 * HEAD, nz * HEAD
    V = pltpu.VMEM
    sem = pltpu.SemaphoreType.DMA
    zl, zsh = ring(nz)
    yl, ysh = ring(ny)
    return pl.pallas_call(
        functools.partial(layer_kernel, ny, nz),
        out_shape=(
            jax.ShapeDtypeStruct(output_cotangent.shape, BF),
            jax.ShapeDtypeStruct(tokens.shape, BF),
        ),
        in_specs=[hbm] * 4,
        out_specs=(vm, vm),
        scratch_shapes=[
            V((4, rows, depth), BF),
            V((4 * depth, n), BF),
            V((HEAD, n), F32),
            V((HEAD, n), F32),
            V((3, depth, n), BF),
            V((4, HEAD, width), BF),
            V((nq, HEAD), BF),
            V((nk, 2 * HEAD), BF),
            V((nq, HEAD), BF),
            V((HEAD, width), BF),
            V((4, HEAD, HEAD), F32),
            V((4, HEAD, HEAD), F32),
            V((HEAD, HEAD), F32),
            V((nk, nq), F32),
            V((nk, nq), F32),
            V((nz, HEAD, HEAD), BF),
            V((nz, HEAD, HEAD), BF),
            V((3, nz, HEAD), F32),
            V((nz, 3, nz, HEAD), F32),
            V((8, nq), F32),
            V((HEAD, nq), F32),
            V((nz, nz, HEAD), F32),
            V((nz, 16, HEAD), F32),
            V((4, HEAD, HEAD), BF),
            V((nz, HEAD, HEAD), BF),
            V((nz, HEAD, HEAD), BF),
            V((nk, 2 * HEAD), F32),
            V((nk, 2 * HEAD), BF),
            V((nk, 2 * HEAD), BF),
            V((4, 2 * HEAD, n), BF),
            V(tokens.shape, F32),
            sem((4,)),
            sem((3, 2)),
            sem((3, 2)),
            sem((2, zl + 1)),
            sem((2, zl + 1)),
            sem((nz, 2, yl + 1)),
            sem((nz, 2, yl + 1)),
            sem((2, zl + 1)),
            sem((2, zl + 1)),
            sem((2,)),
            sem((2,)),
            sem((3, CHUNKS)),
            sem((3, CHUNKS)),
            sem((CHUNKS // 2,)),
            sem((CHUNKS // 2,)),
            sem((CHUNKS // 2, nz)),
            sem((CHUNKS // 2, nz)),
            sem((5, nz)),
            sem((5, nz)),
            sem((CHUNKS // 2, 2 * ny + 1)),
            sem((CHUNKS // 2, 2 * ny + 1)),
            sem((2, 4)),
            sem((2, 4)),
            sem((ny, 2)),
            sem((2 * ny,)),
            sem((2, 7)),
            sem((2, 7)),
        ],
        compiler_params=pltpu.CompilerParams(
            collective_id=0, has_side_effects=True, vmem_limit_bytes=52 * 2**20
        ),
        cost_estimate=pl.CostEstimate(
            flops=6_000_000_000, bytes_accessed=20_000_000, transcendentals=2_000_000
        ),
        name="layer",
    )(tokens, input_weight, output_weight, output_cotangent)


def solution(mesh):
    seq = mesh.shape["seq"]
    nz = 8 if seq % 32 == 0 else seq // 2
    return jax.shard_map(
        functools.partial(body, nz),
        mesh=mesh,
        in_specs=(
            P("seq", ("row", "col")),
            P("row", "col"),
            P("col", None),
            P(("seq", "row"), "col"),
        ),
        out_specs=(P(("seq", "row"), "col"), P("seq", ("row", "col"))),
        check_vma=False,
    )
```
